128 devices in a mesh: space: 16 (over y_lo, z, core), filt: 8 (over y_hi, x).
Axes of the slice: x: 4, y: 4 (y_hi: 2, y_lo: 2; y = y_hi * 2 + y_lo), z: 4, core: 2. Of those that a mesh axis runs over, the one named last changes fastest.
Arguments:
- inputs: bfloat16 [2, 64, 128, 128, 128], P(None, None, 'space', 'filt'), may hold values from -6 to 6
- kernel_one: bfloat16 [3, 3, 3, 64, 128], replicated, may hold values from -0.15625 to 0.15625
- kernel_two: bfloat16 [3, 3, 3, 128, 256], P(None, None, None, None, 'filt'), may hold values from -0.109375 to 0.109375
- cotangent: bfloat16 [2, 256, 32, 1024], P(None, 'filt', 'space'), may hold values from -0.023925781 to 0.023925781
Outputs:
- activation: bfloat16 [2, 256, 32, 1024], P(None, 'filt', 'space')
- grad_one: float32 [3, 3, 3, 64, 128], replicated
- grad_two: float32 [3, 3, 3, 128, 256], P(None, None, None, None, 'filt')
The draws below stay inside these ranges and needn't reach their ends.
All inputs are finite; a program needn't handle non-finite values.
Results may differ from the reference program's by a relative error of at most 0.03.
The reference program's roundings to bfloat16 on the way (of `hidden`, `delta_two` and `delta_one`) count: a program that leaves them out, or rounds other values in their place, can miss the bound.
Values may be sent and summed in bfloat16 or wider, within the bound.
No kernel may reach another device: no remote copies, remote signals or barrier semaphores. Data moves between devices by JAX's collectives and lax.ppermute only.
A program may use at most 192 MiB of HBM per device.

```python
import jax
import jax.numpy as jnp
from jax import lax

C0 = 64
C1 = 128
C2 = 256
SAMPLES = 2
WIDTH = 128
DEPTH = 128
HEIGHT = 128
D2 = 32
H2 = 32
W2 = 32


def block_levels(stream_key, shape, split, least, largest):
    def one(position, shards_of):
        draws = jax.random.uniform(jax.random.fold_in(jax.random.fold_in(stream_key, 6), position), (shards_of,), jnp.float32, least / len(split), largest / len(split))
        return jnp.repeat(jnp.exp(draws), shape[position] // shards_of).reshape((-1,) + (1,) * (len(shape) - position - 1))

    factor_of = one(*split[0])
    for cut in split[1:]:
        factor_of = factor_of * one(*cut)
    return factor_of


def gaussian(key, shape, width, reach, split=(), held_as=jnp.bfloat16):
    drawn = width * jax.random.normal(key, shape, jnp.float32)
    if split:
        drawn = drawn * block_levels(key, shape, split, -0.22, 0.18)
    return jnp.clip(drawn, -reach, reach).astype(held_as)


def setup_inputs(seed: int = 0) -> dict:
    arg_keys = jax.random.split(jax.random.key(seed), 5)
    inputs = gaussian(arg_keys[0], (SAMPLES, C0, DEPTH, HEIGHT, WIDTH), 1.0, 6.0, ((2, 16), (3, 8)))
    kernel_one = gaussian(arg_keys[1], (3, 3, 3, C0, C1), (27 * C0) ** -0.5, 0.15625)
    kernel_two = gaussian(arg_keys[2], (3, 3, 3, C1, C2), (27 * C1) ** -0.5, 0.109375, ((4, 8),))
    cotangent = gaussian(arg_keys[3], (SAMPLES, C2, D2, H2 * W2), 0.004, 0.023925781, ((1, 8), (2, 16)))
    return dict(inputs=inputs, kernel_one=kernel_one, kernel_two=kernel_two, cotangent=cotangent)


def conv_wide(field, kernel):
    return lax.conv_general_dilated(field, kernel, (2, 2, 2), ((1, 1), (1, 1), (1, 1)), dimension_numbers=('NCDHW', 'DHWIO', 'NCDHW'), precision=lax.Precision.HIGHEST)

def leaky(value):
    return jnp.where(value > 0, value, 0.3 * value)

def slope_of(value):
    return jnp.where(value > 0, 1.0, 0.3).astype(value.dtype)

def rounded(value):
    narrow = lax.optimization_barrier(value.astype(jnp.bfloat16))
    return narrow.astype(jnp.float32)

def reference(inputs, kernel_one, kernel_two, cotangent):
    wide_in = inputs.astype(jnp.float32)
    wide_one = kernel_one.astype(jnp.float32)
    wide_two = kernel_two.astype(jnp.float32)
    pre_one = conv_wide(wide_in, wide_one)
    hidden = rounded(leaky(pre_one))
    pre_two, pull_two = jax.vjp(conv_wide, hidden, wide_two)
    shape_two = pre_two.shape
    activation = leaky(pre_two).astype(jnp.bfloat16).reshape(cotangent.shape)
    delta_two = rounded(cotangent.astype(jnp.float32).reshape(shape_two) * slope_of(pre_two))
    back_one, grad_two = pull_two(delta_two)
    delta_one = rounded(back_one * slope_of(pre_one))
    unused, pull_one = jax.vjp(lambda kernel: conv_wide(wide_in, kernel), wide_one)
    grad_one = pull_one(delta_one)[0]
    return (activation, grad_one.astype(jnp.float32), grad_two.astype(jnp.float32))
```

```python
import jax
import jax.numpy as jnp
import numpy as np
from jax import lax
from jax.experimental import pallas as pl
from jax.experimental.pallas import tpu as pltpu
from jax.sharding import PartitionSpec as P

BF = jnp.bfloat16
F32 = jnp.float32
MIB = 1 << 20
LANES = (((1,), (1,)), ((), ()))
PLAIN = (((1,), (0,)), ((), ()))


def params(mib):
    return pltpu.CompilerParams(vmem_limit_bytes=mib * MIB)


def vmem(count):
    return [pl.BlockSpec(memory_space=pltpu.VMEM)] * count


def dot(a, b, dims=PLAIN):
    return lax.dot_general(a, b, dims, preferred_element_type=F32)


def selection():
    rows = np.arange(192)
    column = 2 * (rows % 32) + (rows % 64) // 32
    wanted = 2 * column + rows // 64 - 1
    return (wanted[:, None] == np.arange(128)[None, :]).astype(np.float32)


def spread(sel, rows):
    return dot(sel, rows, LANES).astype(BF)


def split_kernel(x_ref, sel_ref, q_ref, wide):
    wide[...] = x_ref[...].reshape(2048, 128).astype(F32)
    sel = sel_ref[...]
    for k in range(8):
        pair = [wide[pl.ds(2 * k + p, 128, stride=16), :].astype(BF) for p in range(2)]
        both = spread(sel, jnp.concatenate(pair, 0))
        for p in range(2):
            q_ref[0, p, k] = both[:, 128 * p : 128 * p + 128].reshape(3, 64, 128)


def split(inputs, sel):
    return pl.pallas_call(
        split_kernel,
        grid=(8,),
        in_specs=[
            pl.BlockSpec((2, 64, 1, 16, 128), lambda d: (0, 0, d, 0, 0)),
            pl.BlockSpec((192, 128), lambda d: (0, 0)),
        ],
        out_specs=pl.BlockSpec((1, 2, 8, 3, 64, 128), lambda d: (d, 0, 0, 0, 0, 0)),
        out_shape=jax.ShapeDtypeStruct((8, 2, 8, 3, 64, 128), BF),
        scratch_shapes=[pltpu.VMEM((2048, 128), F32)],
        compiler_params=params(32),
        cost_estimate=pl.CostEstimate(flops=1 << 30, bytes_accessed=11 << 20, transcendentals=0),
        name="split_width",
    )(inputs, sel)


def field_rows(q_ref, qd_ref, qr_ref, a, t, u, v):
    d = 2 * a + t - 1
    if d < 0:
        piece = {0: qd_ref[0:8, v], 1: qd_ref[9:17, v], 2: qd_ref[1:9, v]}[u]
    elif u == 0:
        piece = jnp.concatenate([qr_ref[d, v][None], q_ref[d, 1, 0:7, v]], 0)
    else:
        piece = q_ref[d, u - 1, :, v]
    return piece.reshape(512, 128)


def first_kernel(q_ref, xd_ref, xr_ref, sel_ref, k_ref, h_ref, qd_ref, qr_ref, w_ref):
    sel = sel_ref[...]
    for k in range(17):
        qd_ref[k] = spread(sel, xd_ref[k]).reshape(3, 64, 128)
    for k in range(8):
        qr_ref[k] = spread(sel, xr_ref[k]).reshape(3, 64, 128)
    w_ref[...] = jnp.zeros_like(w_ref)
    for k in range(27):
        w_ref[k * 128 : k * 128 + 64, 0:128] = k_ref[k]
        w_ref[k * 128 + 64 : k * 128 + 128, 128:256] = k_ref[k]
    for a in range(4):
        taps = [field_rows(q_ref, qd_ref, qr_ref, a, t, u, v) for t in range(3) for u in range(3) for v in range(3)]
        pre = dot(jnp.concatenate(taps, 1), w_ref[...])
        h_ref[a] = jnp.where(pre > 0, pre, 0.3 * pre).astype(BF).reshape(8, 64, 256)


def first(q, xd, xr, sel, kernel):
    return pl.pallas_call(
        first_kernel,
        in_specs=vmem(5),
        out_specs=vmem(3),
        out_shape=(
            jax.ShapeDtypeStruct((4, 8, 64, 256), BF),
            jax.ShapeDtypeStruct((17, 3, 64, 128), BF),
            jax.ShapeDtypeStruct((8, 3, 64, 128), BF),
        ),
        scratch_shapes=[pltpu.VMEM((27 * 128, 256), BF)],
        compiler_params=params(40),
        name="first_layer",
    )(q, xd, xr, sel, kernel)


def hidden_part(h_ref, hd_ref, hr_ref, hc_ref, a, b):
    if a < 0 and b < 0:
        return hc_ref
    if a < 0:
        return hd_ref.at[b]
    if b < 0:
        return hr_ref.at[a]
    return h_ref.at[a, b]


def shift_rows(value, by):
    wide = pltpu.roll(value.astype(F32), by % 32, 0)
    row = lax.broadcasted_iota(jnp.int32, wide.shape, 0)
    keep = row >= by if by > 0 else row < 32 + by
    return jnp.where(keep, wide, 0.0).astype(BF)


def hidden_shifts(parts, hs_ref):
    for a in range(-1, 4):
        for b in range(-1, 8):
            hs_ref[a + 1, b + 1] = shift_rows(hidden_part(*parts, a, b)[32:64, :], 1)


def hidden_rows(parts, hs_ref, t, u, v):
    pieces = []
    for n in range(2):
        for a in range(2):
            for b in range(4):
                i, j = 2 * a + t - 1, 2 * b + u - 1
                cut = slice(128 * n, 128 * n + 128)
                if v == 0:
                    pieces.append(hs_ref[i + 1, j + 1, :, cut])
                else:
                    pieces.append(hidden_part(*parts, i, j)[32 * (v - 1) : 32 * v, cut])
    return jnp.concatenate(pieces, 0)


def tap_weight(w_ref, k):
    return w_ref[:, 32 * k : 32 * k + 32, :].reshape(256, 128)


def eye(size):
    rows = lax.broadcasted_iota(jnp.int32, (size, size), 0)
    return (rows == lax.broadcasted_iota(jnp.int32, (size, size), 1)).astype(F32).astype(BF)


def second_kernel(h_ref, hd_ref, hr_ref, hc_ref, w_ref, g_ref, act_ref, delta_ref, turned_ref, hs_ref):
    parts = (h_ref, hd_ref, hr_ref, hc_ref)
    hidden_shifts(parts, hs_ref)
    keys = [(t, u, v) for t in range(3) for u in range(3) for v in range(3)]
    left = jnp.concatenate([hidden_rows(parts, hs_ref, *key) for key in keys], 1)
    right = jnp.concatenate([tap_weight(w_ref, k) for k in range(27)], 1)
    pre = dot(left, right, LANES)
    act = jnp.where(pre > 0, pre, 0.3 * pre).astype(BF)
    slope = jnp.where(pre > 0, 1.0, 0.3).astype(F32)
    small, large = eye(128), eye(256)
    for n in range(2):
        for a in range(2):
            at = 256 * n + 128 * a
            rows = slice(at, at + 128)
            act_ref[:, a, n] = dot(large, act[rows], LANES).astype(BF).reshape(8, 32, 128)
            came = dot(small, g_ref[:, a, n].reshape(256, 128), LANES)
            delta = (came * slope[rows]).astype(BF)
            delta_ref[n, a] = delta.reshape(4, 32, 256)
            turned_ref[:, rows] = dot(large, delta, LANES).astype(BF)


def second(h, hd, hr, hc, w, g):
    return pl.pallas_call(
        second_kernel,
        in_specs=vmem(6),
        out_specs=vmem(3),
        out_shape=(
            jax.ShapeDtypeStruct((8, 2, 2, 32, 128), BF),
            jax.ShapeDtypeStruct((2, 2, 4, 32, 256), BF),
            jax.ShapeDtypeStruct((256, 512), BF),
        ),
        scratch_shapes=[pltpu.VMEM((5, 9, 32, 256), BF)],
        compiler_params=params(40),
        name="second_layer",
    )(h, hd, hr, hc, w, g)


def second_grad_kernel(h_ref, hd_ref, hr_ref, hc_ref, turned_ref, out_ref, hs_ref):
    parts = (h_ref, hd_ref, hr_ref, hc_ref)
    hidden_shifts(parts, hs_ref)
    turned = turned_ref[...]
    keys = [(t, u, v) for t in range(3) for u in range(3) for v in range(3)]
    for k in range(0, 27, 2):
        some = keys[k : k + 2]
        right = jnp.concatenate([hidden_rows(parts, hs_ref, *key) for key in some], 1)
        both = dot(turned, right).astype(BF)
        for p in range(len(some)):
            rows = slice(32 * (k + p), 32 * (k + p) + 32)
            out_ref[:, rows, :] = both[:, 128 * p : 128 * p + 128].reshape(8, 32, 128)


def second_grad(h, hd, hr, hc, turned):
    return pl.pallas_call(
        second_grad_kernel,
        in_specs=vmem(5),
        out_specs=vmem(1)[0],
        out_shape=jax.ShapeDtypeStruct((8, 864, 128), BF),
        scratch_shapes=[pltpu.VMEM((5, 9, 32, 256), BF)],
        compiler_params=params(40),
        name="second_kernel_grad",
    )(h, hd, hr, hc, turned)


def delta_part(d_ref, dd_ref, dr_ref, dc_ref, n, a, b):
    if a > 1 and b > 3:
        return dc_ref.at[n]
    if a > 1:
        return dd_ref.at[n, b]
    if b > 3:
        return dr_ref.at[n, a]
    return d_ref.at[n, a, b]


def back_kernel(d_ref, dd_ref, dr_ref, dc_ref, w_ref, h_ref, out_ref, ds_ref):
    parts = (d_ref, dd_ref, dr_ref, dc_ref)
    for n in range(2):
        for a in range(3):
            for b in range(5):
                ds_ref[n, a, b] = shift_rows(delta_part(*parts, n, a, b)[...], -1)
    nothing = jnp.zeros((256, 128), BF)
    choice = (((1, 0),), ((2, 0), (0, 1)))
    for pa in range(2):
        for pb in range(2):
            left, right = [], []
            for t, i in choice[pa]:
                for u, j in choice[pb]:
                    spots = [(n, a + i, b + j) for n in range(2) for a in range(2) for b in range(4)]
                    left.append(jnp.concatenate([delta_part(*parts, *spot)[...] for spot in spots], 0))
                    left.append(jnp.concatenate([ds_ref[spot] for spot in spots], 0))
                    k = 9 * t + 3 * u
                    right.append(jnp.concatenate([tap_weight(w_ref, k + 1), tap_weight(w_ref, k + 2)], 1))
                    right.append(jnp.concatenate([nothing, tap_weight(w_ref, k)], 1))
            back = dot(jnp.concatenate(left, 1), jnp.concatenate(right, 0))
            for n in range(2):
                for a in range(2):
                    for b in range(4):
                        at = 256 * n + 128 * a + 32 * b
                        for pc in range(2):
                            rows, cut = slice(32 * pc, 32 * pc + 32), slice(128 * n, 128 * n + 128)
                            spot = (2 * a + pa, 2 * b + pb, rows, cut)
                            slope = jnp.where(h_ref[spot].astype(F32) > 0, 1.0, 0.3)
                            value = back[at : at + 32, 128 * pc : 128 * pc + 128]
                            out_ref[spot] = (value * slope).astype(BF)


def back(d, dd, dr, dc, w, h):
    return pl.pallas_call(
        back_kernel,
        in_specs=vmem(6),
        out_specs=vmem(1)[0],
        out_shape=jax.ShapeDtypeStruct((4, 8, 64, 256), BF),
        scratch_shapes=[pltpu.VMEM((2, 3, 5, 32, 256), BF)],
        compiler_params=params(40),
        name="back_one",
    )(d, dd, dr, dc, w, h)


def first_grad_kernel(d_ref, q_ref, qd_ref, qr_ref, out_ref, turned_ref):
    large = eye(256)
    for a in range(4):
        turned_ref[:, 512 * a : 512 * a + 512] = dot(large, d_ref[a].reshape(512, 256), LANES).astype(BF)
    keys = [(t, u, v) for t in range(3) for u in range(3) for v in range(3)]
    lane = lax.broadcasted_iota(jnp.int32, (128, 128), 1)
    for k in range(0, 27, 2):
        some = keys[k : k + 2]
        right = [
            jnp.concatenate([field_rows(q_ref, qd_ref, qr_ref, a, *key) for a in range(4)], 0) for key in some
        ]
        both = dot(turned_ref[...], jnp.concatenate(right, 1))
        one = both[0:128, 0:128] + pltpu.roll(both[128:256, 0:128], 64, 1)
        if len(some) == 2:
            two = both[128:256, 128:256] + pltpu.roll(both[0:128, 128:256], 64, 1)
        else:
            two = jnp.zeros_like(one)
        out_ref[64 * k : 64 * k + 128, :] = jnp.where(lane < 64, one, two).T.astype(BF)
    out_ref[1792:2048, :] = jnp.zeros((256, 128), BF)


def first_grad(d, q, qd, qr):
    return pl.pallas_call(
        first_grad_kernel,
        in_specs=vmem(4),
        out_specs=vmem(1)[0],
        out_shape=jax.ShapeDtypeStruct((2048, 128), BF),
        scratch_shapes=[pltpu.VMEM((256, 2048), BF)],
        compiler_params=params(40),
        name="first_kernel_grad",
    )(d, q, qd, qr)


def exchange(value, axes):
    return lax.all_to_all(value, axes, 0, 0, tiled=True)


def everywhere(value, axis):
    devices = lax.axis_size(axis)
    return exchange(jnp.broadcast_to(value[None], (devices,) + value.shape), axis)


def shifted(value, depth, height):
    deep, high = lax.axis_size("space"), lax.axis_size("filt")
    pairs = [
        (i * high + j, (i + depth) * high + j + height)
        for i in range(deep)
        for j in range(high)
        if 0 <= i + depth < deep and 0 <= j + height < high
    ]
    return lax.ppermute(value, ("space", "filt"), pairs)


def body(inputs, kernel_one, kernel_two, cotangent):
    sel = jnp.asarray(selection(), BF)
    last = jnp.transpose(inputs[:, :, 7], (2, 0, 1, 3)).reshape(16, 128, 128)
    side = jnp.transpose(inputs[:, :, :, 15], (2, 0, 1, 3)).reshape(8, 128, 128)
    order = list(range(1, 16, 2)) + list(range(0, 16, 2))
    rim_depth = shifted(jnp.concatenate([last[k : k + 1] for k in order], 0), 1, 0)
    rim_corner = shifted(last[15:16], 1, 1)
    rim_side = shifted(side, 0, 1)
    own = jnp.transpose(kernel_two, (0, 1, 2, 4, 3)).reshape(864, 128)
    parts = jnp.transpose(cotangent.reshape(2, 32, 2, 8, 128), (3, 2, 0, 1, 4)).reshape(8, 128, 128)
    mixed = exchange(jnp.concatenate([jnp.broadcast_to(own[None], (8, 864, 128)), parts], 1), "filt")
    weight, grad_in = mixed[:, :864], mixed[:, 864:].reshape(8, 2, 2, 32, 128)

    q = split(inputs, sel)
    h, qd, qr = first(
        q, jnp.concatenate([rim_corner, rim_depth], 0), rim_side, sel, kernel_one.reshape(27, 64, 128)
    )
    hd, hr, hc = shifted(h[3], 1, 0), shifted(h[:, 7], 0, 1), shifted(h[3, 7], 1, 1)
    act, delta, turned = second(h, hd, hr, hc, weight, grad_in)
    dd, dr, dc = shifted(delta[:, 0], -1, 0), shifted(delta[:, :, 0], 0, -1), shifted(delta[:, 0, 0], -1, -1)
    grad_two = second_grad(h, hd, hr, hc, turned)
    delta_one = back(delta, dd, dr, dc, weight, h)
    grad_one = first_grad(delta_one, q, qd, qr)

    two = jnp.transpose(grad_two.reshape(8, 16, 54, 128), (1, 0, 2, 3)).reshape(128, 54, 128)
    one = grad_one.reshape(128, 16, 128)
    came = exchange(jnp.concatenate([two, one], 1), ("space", "filt"))
    total = jnp.sum(came.astype(F32), 0).astype(BF)
    one = everywhere(total[54:], "filt").reshape(128, 128)
    full = everywhere(jnp.concatenate([total[:54], one], 0), "space")
    grad_two = jnp.transpose(full[:, :54].reshape(3, 3, 3, 32, 128), (0, 1, 2, 4, 3)).astype(F32)
    grad_one = full[:, 54:].reshape(2048, 128)[:1728].reshape(3, 3, 3, 64, 128).astype(F32)

    act = exchange(act, "filt").reshape(8, 2, 2, 32, 128)
    activation = jnp.transpose(act, (2, 3, 1, 0, 4)).reshape(cotangent.shape)
    return (activation, grad_one, grad_two)


def solution(mesh):
    in_specs = (
        P(None, None, "space", "filt", None),
        P(),
        P(None, None, None, None, "filt"),
        P(None, "filt", "space", None),
    )
    out_specs = (P(None, "filt", "space", None), P(), P(None, None, None, None, "filt"))
    return jax.shard_map(body, mesh=mesh, in_specs=in_specs, out_specs=out_specs, check_vma=False)
```

```python
import jax
import jax.numpy as jnp
import numpy as np
from jax import lax
from jax.experimental import pallas as pl
from jax.experimental.pallas import tpu as pltpu
from jax.sharding import PartitionSpec as P

BF = jnp.bfloat16
F32 = jnp.float32
MIB = 1 << 20
LANES = (((1,), (1,)), ((), ()))
PLAIN = (((1,), (0,)), ((), ()))


def params(mib):
    return pltpu.CompilerParams(vmem_limit_bytes=mib * MIB)


def cost(gigaflops, mib):
    return pl.CostEstimate(flops=gigaflops << 30, bytes_accessed=mib * MIB, transcendentals=0)


def vmem(count):
    return [pl.BlockSpec(memory_space=pltpu.VMEM)] * count


SCALAR = pl.BlockSpec(memory_space=pltpu.SMEM)


def dot(a, b, dims=PLAIN):
    return lax.dot_general(a, b, dims, preferred_element_type=F32)


def selection():
    rows = np.arange(192)
    column = 2 * (rows % 32) + (rows % 64) // 32
    wanted = 2 * column + rows // 64 - 1
    return (wanted[:, None] == np.arange(128)[None, :]).astype(np.float32)


def spread(sel, rows):
    return dot(sel, rows, LANES).astype(BF)


def split_kernel(x_ref, sel_ref, q_ref, wide):
    wide[...] = x_ref[...].reshape(2048, 128).astype(F32)
    sel = sel_ref[...]
    for k in range(8):
        pair = [wide[pl.ds(2 * k + p, 128, stride=16), :].astype(BF) for p in range(2)]
        both = spread(sel, jnp.concatenate(pair, 0))
        for p in range(2):
            q_ref[0, p, k] = both[:, 128 * p : 128 * p + 128].reshape(3, 64, 128)


def split(inputs, sel):
    return pl.pallas_call(
        split_kernel,
        grid=(8,),
        in_specs=[
            pl.BlockSpec((2, 64, 1, 16, 128), lambda d: (0, 0, d, 0, 0)),
            pl.BlockSpec((192, 128), lambda d: (0, 0)),
        ],
        out_specs=pl.BlockSpec((1, 2, 8, 3, 64, 128), lambda d: (d, 0, 0, 0, 0, 0)),
        out_shape=jax.ShapeDtypeStruct((8, 2, 8, 3, 64, 128), BF),
        scratch_shapes=[pltpu.VMEM((2048, 128), F32)],
        compiler_params=params(32),
        cost_estimate=cost(2, 11),
        name="split_width",
    )(inputs, sel)


def field_rows(q_ref, qd_ref, qr_ref, a, t, u, v):
    d = 2 * a + t - 1
    if d < 0:
        piece = {0: qd_ref[0:8, v], 1: qd_ref[9:17, v], 2: qd_ref[1:9, v]}[u]
    elif u == 0:
        piece = jnp.concatenate([qr_ref[d, v][None], q_ref[d, 1, 0:7, v]], 0)
    else:
        piece = q_ref[d, u - 1, :, v]
    return piece.reshape(512, 128)


def first_kernel(q_ref, xd_ref, xr_ref, sel_ref, k_ref, h_ref, qd_ref, qr_ref, w_ref):
    sel = sel_ref[...]
    for k in range(17):
        qd_ref[k] = spread(sel, xd_ref[k]).reshape(3, 64, 128)
    for k in range(8):
        qr_ref[k] = spread(sel, xr_ref[k]).reshape(3, 64, 128)
    w_ref[...] = jnp.zeros_like(w_ref)
    for k in range(27):
        w_ref[k * 128 : k * 128 + 64, 0:128] = k_ref[k]
        w_ref[k * 128 + 64 : k * 128 + 128, 128:256] = k_ref[k]
    for a in range(4):
        taps = [field_rows(q_ref, qd_ref, qr_ref, a, t, u, v) for t in range(3) for u in range(3) for v in range(3)]
        pre = dot(jnp.concatenate(taps, 1), w_ref[...])
        h_ref[a] = jnp.where(pre > 0, pre, 0.3 * pre).astype(BF).reshape(8, 64, 256)


def first(q, xd, xr, sel, kernel):
    return pl.pallas_call(
        first_kernel,
        in_specs=vmem(5),
        out_specs=vmem(3),
        out_shape=(
            jax.ShapeDtypeStruct((4, 8, 64, 256), BF),
            jax.ShapeDtypeStruct((17, 3, 64, 128), BF),
            jax.ShapeDtypeStruct((8, 3, 64, 128), BF),
        ),
        scratch_shapes=[pltpu.VMEM((27 * 128, 256), BF)],
        compiler_params=params(40),
        cost_estimate=cost(4, 10),
        name="first_layer",
    )(q, xd, xr, sel, kernel)


def hidden_part(h_ref, hd_ref, hr_ref, hc_ref, a, b):
    if a < 0 and b < 0:
        return hc_ref
    if a < 0:
        return hd_ref.at[b]
    if b < 0:
        return hr_ref.at[a]
    return h_ref.at[a, b]


def shift_rows(value, by):
    wide = pltpu.roll(value.astype(F32), by % 32, 0)
    row = lax.broadcasted_iota(jnp.int32, wide.shape, 0)
    keep = row >= by if by > 0 else row < 32 + by
    return jnp.where(keep, wide, 0.0).astype(BF)


def hidden_shifts(parts, hs_ref):
    for a in range(-1, 4):
        for b in range(-1, 8):
            hs_ref[a + 1, b + 1] = shift_rows(hidden_part(*parts, a, b)[32:64, :], 1)


def hidden_rows(parts, hs_ref, t, u, v):
    pieces = []
    for n in range(2):
        for a in range(2):
            for b in range(4):
                i, j = 2 * a + t - 1, 2 * b + u - 1
                cut = slice(128 * n, 128 * n + 128)
                if v == 0:
                    pieces.append(hs_ref[i + 1, j + 1, :, cut])
                else:
                    pieces.append(hidden_part(*parts, i, j)[32 * (v - 1) : 32 * v, cut])
    return jnp.concatenate(pieces, 0)


def tap_weight(w_ref, k):
    return w_ref[:, 32 * k : 32 * k + 32, :].reshape(256, 128)


def eye(size):
    rows = lax.broadcasted_iota(jnp.int32, (size, size), 0)
    return (rows == lax.broadcasted_iota(jnp.int32, (size, size), 1)).astype(F32).astype(BF)


def second_kernel(h_ref, hd_ref, hr_ref, hc_ref, w_ref, act_ref, delta_ref, turned_ref, hs_ref):
    parts = (h_ref, hd_ref, hr_ref, hc_ref)
    hidden_shifts(parts, hs_ref)
    keys = [(t, u, v) for t in range(3) for u in range(3) for v in range(3)]
    left = jnp.concatenate([hidden_rows(parts, hs_ref, *key) for key in keys], 1)
    right = jnp.concatenate([tap_weight(w_ref, k) for k in range(27)], 1)
    pre = dot(left, right, LANES)
    act = jnp.where(pre > 0, pre, 0.3 * pre).astype(BF)
    slope = jnp.where(pre > 0, 1.0, 0.3).astype(F32)
    small, large = eye(128), eye(256)
    for n in range(2):
        for a in range(2):
            at = 256 * n + 128 * a
            rows = slice(at, at + 128)
            some = slice(64 * a + 32 * n, 32 + 64 * a + 32 * n)
            act_ref[:, some, :] = dot(large, act[rows], LANES).astype(BF).reshape(8, 32, 128)
            some = slice(864 + 64 * a + 32 * n, 896 + 64 * a + 32 * n)
            came = dot(small, w_ref[:, some, :].reshape(256, 128), LANES)
            delta = (came * slope[rows]).astype(BF)
            delta_ref[n, a] = delta.reshape(4, 32, 256)
            turned_ref[:, rows] = dot(large, delta, LANES).astype(BF)


def second(h, hd, hr, hc, w):
    return pl.pallas_call(
        second_kernel,
        in_specs=vmem(5),
        out_specs=vmem(3),
        out_shape=(
            jax.ShapeDtypeStruct((8, 128, 128), BF),
            jax.ShapeDtypeStruct((2, 2, 4, 32, 256), BF),
            jax.ShapeDtypeStruct((256, 512), BF),
        ),
        scratch_shapes=[pltpu.VMEM((5, 9, 32, 256), BF)],
        compiler_params=params(40),
        cost_estimate=cost(1, 4),
        name="second_layer",
    )(h, hd, hr, hc, w)


def second_grad_kernel(core_ref, h_ref, hd_ref, hr_ref, hc_ref, turned_ref, keep_ref, send_ref, hs_ref):
    parts = (h_ref, hd_ref, hr_ref, hc_ref)
    hidden_shifts(parts, hs_ref)
    turned = turned_ref[...]
    even = core_ref[0] == 0
    keys = [(t, u, v) for t in range(3) for u in range(3) for v in range(3)]
    for k in range(0, 27, 2):
        some = keys[k : k + 2]
        right = jnp.concatenate([hidden_rows(parts, hs_ref, *key) for key in some], 1)
        both = dot(turned, right)
        for p in range(len(some)):
            one = both[:, 128 * p : 128 * p + 128].reshape(8, 2, 16, 128)
            low, high = one[:, 0], one[:, 1]
            spot = ((k + p) // 4, slice(None), slice(16 * ((k + p) % 4), 16 * ((k + p) % 4) + 16))
            keep_ref[spot] = jnp.where(even, low, high).astype(BF)
            send_ref[spot] = jnp.where(even, high, low).astype(BF)
    for ref in (keep_ref, send_ref):
        ref[6, :, 48:64] = jnp.zeros((8, 16, 128), BF)
        ref[7] = jnp.zeros((8, 64, 128), BF)


def second_grad(core, h, hd, hr, hc, turned):
    return pl.pallas_call(
        second_grad_kernel,
        in_specs=[SCALAR] + vmem(5),
        out_specs=vmem(2),
        out_shape=(jax.ShapeDtypeStruct((8, 8, 64, 128), BF),) * 2,
        scratch_shapes=[pltpu.VMEM((5, 9, 32, 256), BF)],
        compiler_params=params(40),
        cost_estimate=cost(1, 4),
        name="second_kernel_grad",
    )(core, h, hd, hr, hc, turned)


def delta_part(d_ref, dd_ref, dr_ref, dc_ref, n, a, b):
    if a > 1 and b > 3:
        return dc_ref.at[n]
    if a > 1:
        return dd_ref.at[n, b]
    if b > 3:
        return dr_ref.at[n, a]
    return d_ref.at[n, a, b]


def back_kernel(d_ref, dd_ref, dr_ref, dc_ref, w_ref, h_ref, out_ref, ds_ref):
    parts = (d_ref, dd_ref, dr_ref, dc_ref)
    for n in range(2):
        for a in range(3):
            for b in range(5):
                ds_ref[n, a, b] = shift_rows(delta_part(*parts, n, a, b)[...], -1)
    nothing = jnp.zeros((256, 128), BF)
    choice = (((1, 0),), ((2, 0), (0, 1)))
    for pa in range(2):
        for pb in range(2):
            left, right = [], []
            for t, i in choice[pa]:
                for u, j in choice[pb]:
                    spots = [(n, a + i, b + j) for n in range(2) for a in range(2) for b in range(4)]
                    left.append(jnp.concatenate([delta_part(*parts, *spot)[...] for spot in spots], 0))
                    left.append(jnp.concatenate([ds_ref[spot] for spot in spots], 0))
                    k = 9 * t + 3 * u
                    right.append(jnp.concatenate([tap_weight(w_ref, k + 1), tap_weight(w_ref, k + 2)], 1))
                    right.append(jnp.concatenate([nothing, tap_weight(w_ref, k)], 1))
            back = dot(jnp.concatenate(left, 1), jnp.concatenate(right, 0))
            for n in range(2):
                for a in range(2):
                    for b in range(4):
                        at = 256 * n + 128 * a + 32 * b
                        for pc in range(2):
                            rows, cut = slice(32 * pc, 32 * pc + 32), slice(128 * n, 128 * n + 128)
                            spot = (2 * a + pa, 2 * b + pb, rows, cut)
                            slope = jnp.where(h_ref[spot].astype(F32) > 0, 1.0, 0.3)
                            value = back[at : at + 32, 128 * pc : 128 * pc + 128]
                            out_ref[spot] = (value * slope).astype(BF)


def back(d, dd, dr, dc, w, h):
    return pl.pallas_call(
        back_kernel,
        in_specs=vmem(6),
        out_specs=vmem(1)[0],
        out_shape=jax.ShapeDtypeStruct((4, 8, 64, 256), BF),
        scratch_shapes=[pltpu.VMEM((2, 3, 5, 32, 256), BF)],
        compiler_params=params(40),
        cost_estimate=cost(1, 5),
        name="back_one",
    )(d, dd, dr, dc, w, h)


def first_grad_kernel(core_ref, d_ref, q_ref, qd_ref, qr_ref, keep_ref, send_ref, turned_ref):
    large = eye(256)
    for a in range(4):
        turned_ref[:, 512 * a : 512 * a + 512] = dot(large, d_ref[a].reshape(512, 256), LANES).astype(BF)
    even = core_ref[0] == 0
    keys = [(t, u, v) for t in range(3) for u in range(3) for v in range(3)]
    lane = lax.broadcasted_iota(jnp.int32, (128, 128), 1)
    for k in range(0, 27, 2):
        some = keys[k : k + 2]
        right = [
            jnp.concatenate([field_rows(q_ref, qd_ref, qr_ref, a, *key) for a in range(4)], 0) for key in some
        ]
        both = dot(turned_ref[...], jnp.concatenate(right, 1))
        one = both[0:128, 0:128] + pltpu.roll(both[128:256, 0:128], 64, 1)
        if len(some) == 2:
            two = both[128:256, 128:256] + pltpu.roll(both[0:128, 128:256], 64, 1)
        else:
            two = jnp.zeros_like(one)
        rows = jnp.where(lane < 64, one, two).T
        for j in range(4):
            low, high = rows[32 * j : 32 * j + 16], rows[32 * j + 16 : 32 * j + 32]
            spot = (k // 4, 2 * (k % 4) + j)
            keep_ref[spot] = jnp.where(even, low, high).astype(BF)
            send_ref[spot] = jnp.where(even, high, low).astype(BF)
    for ref in (keep_ref, send_ref):
        ref[7] = jnp.zeros((8, 16, 128), BF)


def first_grad(core, d, q, qd, qr):
    return pl.pallas_call(
        first_grad_kernel,
        in_specs=[SCALAR] + vmem(4),
        out_specs=vmem(2),
        out_shape=(jax.ShapeDtypeStruct((8, 8, 16, 128), BF),) * 2,
        scratch_shapes=[pltpu.VMEM((256, 2048), BF)],
        compiler_params=params(40),
        cost_estimate=cost(4, 9),
        name="first_kernel_grad",
    )(core, d, q, qd, qr)


SPACE = ("y_lo", "z", "core")
FILT = ("y_hi", "x")
CHIPS = ("y_lo", "z", "y_hi", "x")


def exchange(value, axes):
    return lax.all_to_all(value, axes, 0, 0, tiled=True)


def everywhere(value, axes):
    devices = lax.axis_size(axes)
    return exchange(jnp.broadcast_to(value[None], (devices,) + value.shape), axes)


def total(pieces):
    return jnp.sum(pieces.astype(F32), 0).astype(BF)


def paired(keep, send):
    came = lax.ppermute(send, "core", [(0, 1), (1, 0)])
    return (keep.astype(F32) + came.astype(F32)).astype(BF)


def shifted(value, depth, height):
    deep, high = lax.axis_size(SPACE), lax.axis_size(FILT)
    pairs = [
        (i * high + j, (i + depth) * high + j + height)
        for i in range(deep)
        for j in range(high)
        if 0 <= i + depth < deep and 0 <= j + height < high
    ]
    return lax.ppermute(value, SPACE + FILT, pairs)


def body(inputs, kernel_one, kernel_two, cotangent):
    core = lax.axis_index("core").reshape(1)
    sel = jnp.asarray(selection(), BF)
    last = jnp.transpose(inputs[:, :, 7], (2, 0, 1, 3)).reshape(16, 128, 128)
    side = jnp.transpose(inputs[:, :, :, 15], (2, 0, 1, 3)).reshape(8, 128, 128)
    order = list(range(1, 16, 2)) + list(range(0, 16, 2))
    rim_depth = shifted(jnp.concatenate([last[k : k + 1] for k in order], 0), 1, 0)
    rim_corner = shifted(last[15:16], 1, 1)
    rim_side = shifted(side, 0, 1)
    q = split(inputs, sel)
    own = jnp.transpose(kernel_two, (0, 1, 2, 4, 3)).reshape(864, 128)
    parts = jnp.transpose(cotangent.reshape(2, 32, 2, 8, 128), (3, 2, 0, 1, 4)).reshape(8, 128, 128)
    mixed = jnp.concatenate([jnp.broadcast_to(own[None], (8, 864, 128)), parts], 1)
    mixed, rim_depth, rim_side, rim_corner = lax.optimization_barrier((mixed, rim_depth, rim_side, rim_corner))
    mixed = exchange(mixed, FILT)

    h, qd, qr = first(
        q, jnp.concatenate([rim_corner, rim_depth], 0), rim_side, sel, kernel_one.reshape(27, 64, 128)
    )
    hd, hr, hc = shifted(h[3], 1, 0), shifted(h[:, 7], 0, 1), shifted(h[3, 7], 1, 1)
    act, delta, turned = second(h, hd, hr, hc, mixed)
    dd, dr, dc = shifted(delta[:, 0], -1, 0), shifted(delta[:, :, 0], 0, -1), shifted(delta[:, 0, 0], -1, -1)
    two = second_grad(core, h, hd, hr, hc, turned)
    two, dd, dr, dc = lax.optimization_barrier((two, dd, dr, dc))
    two = paired(*two)
    delta_one = back(delta, dd, dr, dc, mixed, h)
    one = paired(*first_grad(core, delta_one, q, qd, qr))

    both = jnp.concatenate([two, one], 2).reshape(64, 80, 128)
    both = total(exchange(both, CHIPS))
    one = jnp.broadcast_to(both[None, 64:], (8, 16, 128))
    came = exchange(jnp.concatenate([act, one], 1), FILT)
    full = everywhere(jnp.concatenate([both[:64], came[:, 128:].reshape(128, 128)], 0), SPACE)
    two = full[:, :64].reshape(8, 2, 4, 16, 128)
    two = jnp.transpose(two, (0, 2, 1, 3, 4)).reshape(1024, 128)[:864].reshape(3, 3, 3, 32, 128)
    grad_two = jnp.transpose(two, (0, 1, 2, 4, 3)).astype(F32)
    one = full[:, 64:].reshape(8, 2, 8, 16, 128)
    one = jnp.transpose(one, (0, 2, 1, 3, 4)).reshape(2048, 128)[:1728]
    grad_one = one.reshape(3, 3, 3, 64, 128).astype(F32)

    act = came[:, :128].reshape(8, 2, 2, 32, 128)
    activation = jnp.transpose(act, (2, 3, 1, 0, 4)).reshape(cotangent.shape)
    return (activation, grad_one, grad_two)


def solution(mesh):
    fine = jax.sharding.Mesh(mesh.devices.reshape(2, 4, 2, 2, 4), ("y_lo", "z", "core", "y_hi", "x"))
    in_specs = (
        P(None, None, SPACE, FILT, None),
        P(),
        P(None, None, None, None, FILT),
        P(None, FILT, SPACE, None),
    )
    out_specs = (P(None, FILT, SPACE, None), P(), P(None, None, None, None, FILT))
    return jax.shard_map(body, mesh=fine, in_specs=in_specs, out_specs=out_specs, check_vma=False)
```

```python
import jax
import jax.numpy as jnp
import numpy as np
from jax import lax
from jax.experimental import pallas as pl
from jax.experimental.pallas import tpu as pltpu
from jax.sharding import PartitionSpec as P

BF = jnp.bfloat16
F32 = jnp.float32
MIB = 1 << 20
LANES = (((1,), (1,)), ((), ()))
PLAIN = (((1,), (0,)), ((), ()))


def params(mib):
    return pltpu.CompilerParams(vmem_limit_bytes=mib * MIB)


def cost(gigaflops, mib):
    return pl.CostEstimate(flops=gigaflops << 30, bytes_accessed=mib * MIB, transcendentals=0)


def vmem(count):
    return [pl.BlockSpec(memory_space=pltpu.VMEM)] * count


SCALAR = pl.BlockSpec(memory_space=pltpu.SMEM)


def dot(a, b, dims=PLAIN):
    return lax.dot_general(a, b, dims, preferred_element_type=F32)


def selection():
    column = 2 * (np.arange(64) % 32) + np.arange(64) // 32
    wanted = np.concatenate([2 * column[:32] - 1, 2 * column, 2 * column + 1])
    return (wanted[:, None] == np.arange(128)[None, :]).astype(np.float32)


def spread(sel, rows):
    return dot(sel, rows, LANES).astype(BF)


PITCH = 24


def slab_rows(x_ref, d, wide):
    wide[:, 0:16, :] = x_ref[:, :, d].reshape(128, 16, 128).astype(F32)


def row(wide, h):
    return wide.reshape(128 * PITCH, 128)[pl.ds(h, 128, stride=PITCH), :].astype(BF)


def rims_kernel(x_ref, side_ref, last_ref, wide):
    for d in range(8):
        slab_rows(x_ref, d, wide)
        side_ref[d] = row(wide, 15)
    for k in range(8):
        last_ref[k] = row(wide, 2 * k + 1)
        last_ref[8 + k] = row(wide, 2 * k)


def rims_of(inputs):
    return pl.pallas_call(
        rims_kernel,
        in_specs=vmem(1),
        out_specs=vmem(2),
        out_shape=(jax.ShapeDtypeStruct((8, 128, 128), BF), jax.ShapeDtypeStruct((16, 128, 128), BF)),
        scratch_shapes=[pltpu.VMEM((128, PITCH, 128), F32)],
        compiler_params=params(16),
        cost_estimate=cost(0, 6),
        name="input_rims",
    )(inputs)


def mix_kernel(core_ref, own_ref, parts_ref, out_ref):
    even = core_ref[0] == 0
    for k in range(27):
        low, high = own_ref[32 * k : 32 * k + 16], own_ref[32 * k + 16 : 32 * k + 32]
        half = jnp.where(even, low.astype(F32), high.astype(F32)).astype(BF)
        for g in range(8):
            out_ref[g, 16 * k : 16 * k + 16] = half
    for g in range(8):
        out_ref[g, 432:560] = parts_ref[g]


def mix(core, own, parts):
    return pl.pallas_call(
        mix_kernel,
        in_specs=[SCALAR] + vmem(2),
        out_specs=vmem(1)[0],
        out_shape=jax.ShapeDtypeStruct((8, 560, 128), BF),
        compiler_params=params(16),
        cost_estimate=cost(0, 3),
        name="weights_and_cotangent",
    )(core, own, parts)


def field_tile(q_ref, qd_ref, qr_ref, a, b, t, u, v):
    d = 2 * a + t - 1
    if d < 0:
        ref = qd_ref.at[(b, 9 + b, b + 1)[u]]
    elif u == 0:
        ref = q_ref.at[d, 1, b - 1] if b else qr_ref.at[d]
    else:
        ref = q_ref.at[d, u - 1, b]
    if v == 0:
        return jnp.concatenate([ref[0:32, :], ref[96:128, :]], 0)
    return ref[64 * v - 32 : 64 * v + 32, :]


def field_rows(q_ref, qd_ref, qr_ref, a, t, u, v):
    return jnp.concatenate([field_tile(q_ref, qd_ref, qr_ref, a, b, t, u, v) for b in range(8)], 0)


def first_kernel(
    x_ref, xd_ref, xr_ref, xc_ref, sel_ref, k_ref,
    h_ref, q_out, qd_ref, qr_ref, last_ref, side_ref, end_ref,
    x_slabs, q_ref, w_ref, wide, came, went,
):
    def load(d):
        return pltpu.make_async_copy(x_ref.at[:, :, d], x_slabs.at[d], came.at[d])

    def store(d):
        return pltpu.make_async_copy(q_ref.at[d], q_out.at[d], went.at[d])

    for d in range(8):
        load(d).start()
    sel = sel_ref[...]
    qd_ref[0] = spread(sel, xc_ref[...])
    for k in range(16):
        qd_ref[k + 1] = spread(sel, xd_ref[k])
    for k in range(8):
        qr_ref[k] = spread(sel, xr_ref[k])
    w_ref[...] = jnp.zeros_like(w_ref)
    for k in range(27):
        w_ref[k * 128 : k * 128 + 64, 0:128] = k_ref[k]
        w_ref[k * 128 + 64 : k * 128 + 128, 128:256] = k_ref[k]

    @pl.loop(0, 8)
    def slab(d):
        load(d).wait()
        wide[:, 0:16, :] = x_slabs[d].reshape(128, 16, 128).astype(F32)
        for k in range(8):
            both = spread(sel, jnp.concatenate([row(wide, 2 * k), row(wide, 2 * k + 1)], 0))
            for p in range(2):
                q_ref[d, p, k] = both[:, 128 * p : 128 * p + 128]
        store(d).start()

    for a in range(4):
        taps = [field_rows(q_ref, qd_ref, qr_ref, a, t, u, v) for t in range(3) for u in range(3) for v in range(3)]
        pre = dot(jnp.concatenate(taps, 1), w_ref[...])
        out = jnp.where(pre > 0, pre, 0.3 * pre).astype(BF).reshape(8, 64, 256)
        h_ref[a] = out
        side_ref[a] = out[7]
        if a == 3:
            last_ref[...] = out
            end_ref[...] = out[7]
    for d in range(8):
        store(d).wait()


def first(x, xd, xr, xc, sel, kernel):
    anywhere = pl.BlockSpec(memory_space=pl.ANY)
    return pl.pallas_call(
        first_kernel,
        in_specs=[anywhere] + vmem(5),
        out_specs=vmem(1) + [anywhere] + vmem(5),
        out_shape=(
            jax.ShapeDtypeStruct((4, 8, 64, 256), BF),
            jax.ShapeDtypeStruct((8, 2, 8, 160, 128), BF),
            jax.ShapeDtypeStruct((17, 160, 128), BF),
            jax.ShapeDtypeStruct((8, 160, 128), BF),
            jax.ShapeDtypeStruct((8, 64, 256), BF),
            jax.ShapeDtypeStruct((4, 64, 256), BF),
            jax.ShapeDtypeStruct((64, 256), BF),
        ),
        scratch_shapes=[
            pltpu.VMEM((8, 2, 64, 16, 128), BF),
            pltpu.VMEM((8, 2, 8, 160, 128), BF),
            pltpu.VMEM((27 * 128, 256), BF),
            pltpu.VMEM((128, PITCH, 128), F32),
            pltpu.SemaphoreType.DMA((8,)),
            pltpu.SemaphoreType.DMA((8,)),
        ],
        compiler_params=params(56),
        cost_estimate=cost(6, 20),
        name="first_layer",
    )(x, xd, xr, xc, sel, kernel)


def hidden_part(h_ref, hd_ref, hr_ref, hc_ref, a, b):
    if a < 0 and b < 0:
        return hc_ref
    if a < 0:
        return hd_ref.at[b]
    if b < 0:
        return hr_ref.at[a]
    return h_ref.at[a, b]


def shift_rows(value, by):
    wide = pltpu.roll(value.astype(F32), by % 32, 0)
    row = lax.broadcasted_iota(jnp.int32, wide.shape, 0)
    keep = row >= by if by > 0 else row < 32 + by
    return jnp.where(keep, wide, 0.0).astype(BF)


def hidden_shifts(parts, hs_ref):
    for a in range(-1, 4):
        for b in range(-1, 8):
            hs_ref[a + 1, b + 1] = shift_rows(hidden_part(*parts, a, b)[32:64, :], 1)


def hidden_rows(parts, hs_ref, t, u, v):
    pieces = []
    for n in range(2):
        for a in range(2):
            for b in range(4):
                i, j = 2 * a + t - 1, 2 * b + u - 1
                cut = slice(128 * n, 128 * n + 128)
                if v == 0:
                    pieces.append(hs_ref[i + 1, j + 1, :, cut])
                else:
                    pieces.append(hidden_part(*parts, i, j)[32 * (v - 1) : 32 * v, cut])
    return jnp.concatenate(pieces, 0)


WEIGHT = pltpu.VMEM((8, 864, 128), BF)


def whole_weight(core_ref, mine_ref, other_ref, w_ref):
    even = core_ref[0] == 0
    for k in range(27):
        mine, other = (ref[:, 16 * k : 16 * k + 16, :].astype(F32) for ref in (mine_ref, other_ref))
        w_ref[:, 32 * k : 32 * k + 16, :] = jnp.where(even, mine, other).astype(BF)
        w_ref[:, 32 * k + 16 : 32 * k + 32, :] = jnp.where(even, other, mine).astype(BF)


def tap_weight(w_ref, k):
    return w_ref[:, 32 * k : 32 * k + 32, :].reshape(256, 128)


def eye(size):
    rows = lax.broadcasted_iota(jnp.int32, (size, size), 0)
    return (rows == lax.broadcasted_iota(jnp.int32, (size, size), 1)).astype(F32).astype(BF)


def second_kernel(
    core_ref, h_ref, hd_ref, hr_ref, hc_ref, m_ref, o_ref, act_ref, delta_ref, turned_ref, last_ref, side_ref, w_ref, hs_ref
):
    parts = (h_ref, hd_ref, hr_ref, hc_ref)
    hidden_shifts(parts, hs_ref)
    whole_weight(core_ref, m_ref, o_ref, w_ref)
    keys = [(t, u, v) for t in range(3) for u in range(3) for v in range(3)]
    left = jnp.concatenate([hidden_rows(parts, hs_ref, *key) for key in keys], 1)
    right = jnp.concatenate([tap_weight(w_ref, k) for k in range(27)], 1)
    pre = dot(left, right, LANES)
    act = jnp.where(pre > 0, pre, 0.3 * pre).astype(BF)
    slope = jnp.where(pre > 0, 1.0, 0.3).astype(F32)
    small, large = eye(128), eye(256)
    for n in range(2):
        for a in range(2):
            at = 256 * n + 128 * a
            rows = slice(at, at + 128)
            some = slice(64 * a + 32 * n, 32 + 64 * a + 32 * n)
            act_ref[:, some, :] = dot(large, act[rows], LANES).astype(BF).reshape(8, 32, 128)
            some = slice(432 + 64 * a + 32 * n, 464 + 64 * a + 32 * n)
            came = dot(small, m_ref[:, some, :].reshape(256, 128), LANES)
            delta = (came * slope[rows]).astype(BF)
            delta_ref[n, a] = delta.reshape(4, 32, 256)
            side_ref[n, a] = delta[0:32]
            if a == 0:
                last_ref[n] = delta.reshape(4, 32, 256)
            turned_ref[:, rows] = dot(large, delta, LANES).astype(BF)


def second(core, h, hd, hr, hc, mine, other):
    return pl.pallas_call(
        second_kernel,
        in_specs=[SCALAR] + vmem(6),
        out_specs=vmem(5),
        out_shape=(
            jax.ShapeDtypeStruct((8, 128, 128), BF),
            jax.ShapeDtypeStruct((2, 2, 4, 32, 256), BF),
            jax.ShapeDtypeStruct((256, 512), BF),
            jax.ShapeDtypeStruct((2, 4, 32, 256), BF),
            jax.ShapeDtypeStruct((2, 2, 32, 256), BF),
        ),
        scratch_shapes=[WEIGHT, pltpu.VMEM((5, 9, 32, 256), BF)],
        compiler_params=params(40),
        cost_estimate=cost(1, 4),
        name="second_layer",
    )(core, h, hd, hr, hc, mine, other)


def second_grad_kernel(core_ref, h_ref, hd_ref, hr_ref, hc_ref, turned_ref, keep_ref, send_ref, hs_ref):
    parts = (h_ref, hd_ref, hr_ref, hc_ref)
    hidden_shifts(parts, hs_ref)
    turned = turned_ref[...]
    even = core_ref[0] == 0
    keys = [(t, u, v) for t in range(3) for u in range(3) for v in range(3)]
    for k in range(0, 27, 2):
        some = keys[k : k + 2]
        right = jnp.concatenate([hidden_rows(parts, hs_ref, *key) for key in some], 1)
        both = dot(turned, right)
        for p in range(len(some)):
            one = both[:, 128 * p : 128 * p + 128].reshape(8, 2, 16, 128)
            low, high = one[:, 0], one[:, 1]
            spot = ((k + p) // 4, slice(None), slice(16 * ((k + p) % 4), 16 * ((k + p) % 4) + 16))
            keep_ref[spot] = jnp.where(even, low, high).astype(BF)
            send_ref[spot] = jnp.where(even, high, low).astype(BF)
    for ref in (keep_ref, send_ref):
        ref[6, :, 48:64] = jnp.zeros((8, 16, 128), BF)
        ref[7] = jnp.zeros((8, 64, 128), BF)


def second_grad(core, h, hd, hr, hc, turned):
    return pl.pallas_call(
        second_grad_kernel,
        in_specs=[SCALAR] + vmem(5),
        out_specs=vmem(2),
        out_shape=(jax.ShapeDtypeStruct((8, 8, 64, 128), BF),) * 2,
        scratch_shapes=[pltpu.VMEM((5, 9, 32, 256), BF)],
        compiler_params=params(40),
        cost_estimate=cost(1, 4),
        name="second_kernel_grad",
    )(core, h, hd, hr, hc, turned)


def delta_part(d_ref, dd_ref, dr_ref, n, a, b):
    if a > 1:
        return dd_ref.at[n, b]
    if b > 3:
        return dr_ref.at[n, a]
    return d_ref.at[n, a, b]


INNER = [(a, b) for a in range(3) for b in range(7) if (a, b) != (2, 6)]
OUTER = [(3, b) for b in range(8)] + [(0, 7), (1, 7), (2, 7), (2, 6)]


def back_rows(parts, ds_ref, w_ref, h_ref, d_ref, places):
    nothing = jnp.zeros((256, 128), BF)
    choice = (((1, 0),), ((2, 0), (0, 1)))
    for pa in range(2):
        for pb in range(2):
            some = [(a // 2, b // 2) for a, b in places if (a % 2, b % 2) == (pa, pb)]
            left, right = [], []
            for t, i in choice[pa]:
                for u, j in choice[pb]:
                    spots = [(n, a + i, b + j) for n in range(2) for a, b in some]
                    left.append(jnp.concatenate([delta_part(*parts, *spot)[...] for spot in spots], 0))
                    left.append(jnp.concatenate([ds_ref[spot] for spot in spots], 0))
                    k = 9 * t + 3 * u
                    right.append(jnp.concatenate([tap_weight(w_ref, k + 1), tap_weight(w_ref, k + 2)], 1))
                    right.append(jnp.concatenate([nothing, tap_weight(w_ref, k)], 1))
            back = dot(jnp.concatenate(left, 1), jnp.concatenate(right, 0))
            for n in range(2):
                for x, (a, b) in enumerate(some):
                    at = 32 * (n * len(some) + x)
                    place = 2 * a + pa, 2 * b + pb
                    for pc in range(2):
                        rows, cut = slice(32 * pc, 32 * pc + 32), slice(128 * n, 128 * n + 128)
                        slope = jnp.where(h_ref[(*place, rows, cut)].astype(F32) > 0, 1.0, 0.3)
                        value = back[at : at + 32, 128 * pc : 128 * pc + 128]
                        d_ref[places.index(place), rows, cut] = (value * slope).astype(BF)


def grad_rows(d_ref, fields, places):
    turned = dot(eye(256), d_ref[...].reshape(64 * len(places), 256), LANES).astype(BF)
    keys = [(t, u, v) for t in range(3) for u in range(3) for v in range(3)]
    lane = lax.broadcasted_iota(jnp.int32, (128, 128), 1)
    for k in range(0, 27, 2):
        some = keys[k : k + 2]
        right = [jnp.concatenate([field_tile(*fields, *place, *key) for place in places], 0) for key in some]
        both = dot(turned, jnp.concatenate(right, 1))
        one = both[0:128, 0:128] + pltpu.roll(both[128:256, 0:128], 64, 1)
        if len(some) == 2:
            two = both[128:256, 128:256] + pltpu.roll(both[0:128, 128:256], 64, 1)
        else:
            two = jnp.zeros_like(one)
        yield k, jnp.where(lane < 64, one, two).T


def inner_kernel(core_ref, d_ref, m_ref, o_ref, h_ref, q_ref, qd_ref, qr_ref, out_ref, w_ref, ds_ref, one_ref):
    whole_weight(core_ref, m_ref, o_ref, w_ref)
    for n in range(2):
        for a in range(2):
            for b in range(4):
                ds_ref[n, a, b] = shift_rows(d_ref[n, a, b], -1)
    parts = (d_ref, None, None)
    back_rows(parts, ds_ref, w_ref, h_ref, one_ref, INNER)
    for k, rows in grad_rows(one_ref, (q_ref, qd_ref, qr_ref), INNER):
        out_ref[k // 2] = rows


def inner(core, d, mine, other, h, q, qd, qr):
    return pl.pallas_call(
        inner_kernel,
        in_specs=[SCALAR] + vmem(7),
        out_specs=vmem(1)[0],
        out_shape=jax.ShapeDtypeStruct((14, 128, 128), F32),
        scratch_shapes=[WEIGHT, pltpu.VMEM((2, 2, 4, 32, 256), BF), pltpu.VMEM((len(INNER), 64, 256), BF)],
        compiler_params=params(40),
        cost_estimate=cost(4, 9),
        name="first_kernel_grad_inner",
    )(core, d, mine, other, h, q, qd, qr)


def outer_kernel(
    core_ref, d_ref, dd_ref, dr_ref, m_ref, o_ref, h_ref, q_ref, qd_ref, qr_ref, sum_ref,
    keep_ref, send_ref, w_ref, ds_ref, one_ref,
):
    whole_weight(core_ref, m_ref, o_ref, w_ref)
    parts = (d_ref, dd_ref, dr_ref)
    for n in range(2):
        for a in range(3):
            for b in range(5):
                ds_ref[n, a, b] = shift_rows(delta_part(*parts, n, a, b)[...], -1)
    back_rows(parts, ds_ref, w_ref, h_ref, one_ref, OUTER)
    even = core_ref[0] == 0
    for k, rows in grad_rows(one_ref, (q_ref, qd_ref, qr_ref), OUTER):
        rows = rows + sum_ref[k // 2]
        for j in range(4):
            low, high = rows[32 * j : 32 * j + 16], rows[32 * j + 16 : 32 * j + 32]
            spot = (k // 4, 2 * (k % 4) + j)
            keep_ref[spot] = jnp.where(even, low, high).astype(BF)
            send_ref[spot] = jnp.where(even, high, low).astype(BF)
    for ref in (keep_ref, send_ref):
        ref[7] = jnp.zeros((8, 16, 128), BF)


def outer(core, d, dd, dr, mine, other, h, q, qd, qr, partial):
    return pl.pallas_call(
        outer_kernel,
        in_specs=[SCALAR] + vmem(10),
        out_specs=vmem(2),
        out_shape=(jax.ShapeDtypeStruct((8, 8, 16, 128), BF),) * 2,
        scratch_shapes=[WEIGHT, pltpu.VMEM((2, 3, 5, 32, 256), BF), pltpu.VMEM((len(OUTER), 64, 256), BF)],
        compiler_params=params(40),
        cost_estimate=cost(2, 9),
        name="first_kernel_grad",
    )(core, d, dd, dr, mine, other, h, q, qd, qr, partial)


SPACE = ("y_lo", "z", "core")
FILT = ("y_hi", "x")
SLABS = ("y_lo", "z")
CHIPS = ("y_lo", "z", "y_hi", "x")


def exchange(value, axes):
    return lax.all_to_all(value, axes, 0, 0, tiled=True)


def everywhere(value, axes):
    devices = lax.axis_size(axes)
    return exchange(jnp.broadcast_to(value[None], (devices,) + value.shape), axes)


def total(pieces):
    return jnp.sum(pieces.astype(F32), 0).astype(BF)


def paired(keep, send):
    came = lax.ppermute(send, "core", [(0, 1), (1, 0)])
    return (keep.astype(F32) + came.astype(F32)).astype(BF)


def shifted(value, depth, height):
    deep, high = lax.axis_size(SPACE), lax.axis_size(FILT)
    pairs = [
        (i * high + j, (i + depth) * high + j + height)
        for i in range(deep)
        for j in range(high)
        if 0 <= i + depth < deep and 0 <= j + height < high
    ]
    return lax.ppermute(value, SPACE + FILT, pairs)


def body(inputs, kernel_one, kernel_two, cotangent):
    core = lax.axis_index("core").reshape(1)
    sel = jnp.asarray(selection(), BF)
    own = jnp.transpose(kernel_two, (0, 1, 2, 4, 3)).reshape(864, 128)
    parts = jnp.transpose(cotangent.reshape(2, 32, 2, 8, 128), (3, 2, 0, 1, 4)).reshape(8, 128, 128)
    mixed = mix(core, own, parts)

    side, last = rims_of(inputs)
    xr = shifted(side, 0, 1)
    xd = shifted(last, 1, 0)
    xc = shifted(last[7], 1, 1)
    mixed, xr, xd, xc = lax.optimization_barrier((mixed, xr, xd, xc))
    mixed = exchange(mixed, FILT)
    h, q, qd, qr, last, side, end = first(inputs, xd, xr, xc, sel, kernel_one.reshape(27, 64, 128))
    mixed, end = lax.optimization_barrier((mixed, end))
    other = lax.ppermute(mixed, "core", [(0, 1), (1, 0)])
    hr = shifted(side, 0, 1)
    hd = shifted(last, 1, 0)
    hc = shifted(end, 1, 1)
    act, delta, turned, last, side = second(core, h, hd, hr, hc, mixed, other)
    dr = shifted(side, 0, -1)
    partial = inner(core, delta, mixed, other, h, q, qd, qr)
    dr, partial = lax.optimization_barrier((dr, partial))
    dd = shifted(jnp.concatenate([last, dr[:, :1]], 1), -1, 0)
    two = second_grad(core, h, hd, hr, hc, turned)
    two, dd = lax.optimization_barrier((two, dd))
    two = paired(*two)
    one = paired(*outer(core, delta, dd, dr, mixed, other, h, q, qd, qr, partial))

    both = jnp.concatenate([two, one], 2).reshape(64, 80, 128)
    both = total(exchange(both, CHIPS))
    one = jnp.broadcast_to(both[None, 64:], (8, 16, 128))
    came = exchange(jnp.concatenate([act, one], 1), FILT)
    mine = everywhere(jnp.concatenate([both[:64], came[:, 128:].reshape(128, 128)], 0), SLABS)
    other = lax.ppermute(mine, "core", [(0, 1), (1, 0)])
    even = lax.axis_index("core") == 0
    full = jnp.stack([jnp.where(even, mine, other), jnp.where(even, other, mine)], 1)
    two = full[:, :, :64].reshape(8, 2, 4, 16, 128)
    two = jnp.transpose(two, (0, 2, 1, 3, 4)).reshape(1024, 128)[:864].reshape(3, 3, 3, 32, 128)
    grad_two = jnp.transpose(two, (0, 1, 2, 4, 3)).astype(F32)
    one = full[:, :, 64:].reshape(8, 2, 8, 16, 128)
    one = jnp.transpose(one, (0, 2, 1, 3, 4)).reshape(2048, 128)[:1728]
    grad_one = one.reshape(3, 3, 3, 64, 128).astype(F32)

    act = came[:, :128].reshape(8, 2, 2, 32, 128)
    activation = jnp.transpose(act, (2, 3, 1, 0, 4)).reshape(cotangent.shape)
    return (activation, grad_one, grad_two)


def solution(mesh):
    fine = jax.sharding.Mesh(mesh.devices.reshape(2, 4, 2, 2, 4), ("y_lo", "z", "core", "y_hi", "x"))
    in_specs = (
        P(None, None, SPACE, FILT, None),
        P(),
        P(None, None, None, None, FILT),
        P(None, FILT, SPACE, None),
    )
    out_specs = (P(None, FILT, SPACE, None), P(), P(None, None, None, None, FILT))
    return jax.shard_map(body, mesh=fine, in_specs=in_specs, out_specs=out_specs, check_vma=False)
```

```python
import jax
import jax.numpy as jnp
import numpy as np
from jax import lax
from jax.experimental import pallas as pl
from jax.experimental.pallas import tpu as pltpu
from jax.sharding import PartitionSpec as P

BF = jnp.bfloat16
F32 = jnp.float32
MIB = 1 << 20
LANES = (((1,), (1,)), ((), ()))
PLAIN = (((1,), (0,)), ((), ()))


def params(mib):
    return pltpu.CompilerParams(vmem_limit_bytes=mib * MIB)


def cost(gigaflops, mib):
    return pl.CostEstimate(flops=gigaflops << 30, bytes_accessed=mib * MIB, transcendentals=0)


def vmem(count):
    return [pl.BlockSpec(memory_space=pltpu.VMEM)] * count


SCALAR = pl.BlockSpec(memory_space=pltpu.SMEM)


def dot(a, b, dims=PLAIN):
    return lax.dot_general(a, b, dims, preferred_element_type=F32)


def selection():
    column = 2 * (np.arange(64) % 32) + np.arange(64) // 32
    wanted = np.concatenate([2 * column[:32] - 1, 2 * column, 2 * column + 1])
    return (wanted[:, None] == np.arange(128)[None, :]).astype(np.float32)


def spread(sel, rows):
    return dot(sel, rows, LANES).astype(BF)


PITCH = 24


def slab_rows(x_ref, d, wide):
    wide[:, 0:16, :] = x_ref[:, :, d].reshape(128, 16, 128).astype(F32)


def row(wide, h):
    return wide.reshape(128 * PITCH, 128)[pl.ds(h, 128, stride=PITCH), :].astype(BF)


def rims_kernel(x_ref, side_ref, last_ref, wide):
    for d in range(8):
        slab_rows(x_ref, d, wide)
        side_ref[d] = row(wide, 15)
    for k in range(8):
        last_ref[k] = row(wide, 2 * k + 1)
        last_ref[8 + k] = row(wide, 2 * k)


def rims_of(inputs):
    return pl.pallas_call(
        rims_kernel,
        in_specs=vmem(1),
        out_specs=vmem(2),
        out_shape=(jax.ShapeDtypeStruct((8, 128, 128), BF), jax.ShapeDtypeStruct((16, 128, 128), BF)),
        scratch_shapes=[pltpu.VMEM((128, PITCH, 128), F32)],
        compiler_params=params(16),
        cost_estimate=cost(0, 6),
        name="input_rims",
    )(inputs)


def mix_kernel(core_ref, own_ref, parts_ref, out_ref):
    even = core_ref[0] == 0
    for k in range(27):
        low, high = own_ref[32 * k : 32 * k + 16], own_ref[32 * k + 16 : 32 * k + 32]
        half = jnp.where(even, low.astype(F32), high.astype(F32)).astype(BF)
        for g in range(8):
            out_ref[g, 16 * k : 16 * k + 16] = half
    for g in range(8):
        out_ref[g, 432:560] = parts_ref[g]


def mix(core, own, parts):
    return pl.pallas_call(
        mix_kernel,
        in_specs=[SCALAR] + vmem(2),
        out_specs=vmem(1)[0],
        out_shape=jax.ShapeDtypeStruct((8, 560, 128), BF),
        compiler_params=params(16),
        cost_estimate=cost(0, 3),
        name="weights_and_cotangent",
    )(core, own, parts)


def field_tile(q_ref, qd_ref, qr_ref, a, b, t, u, v):
    d = 2 * a + t - 1
    if d < 0:
        ref = qd_ref.at[(b, 9 + b, b + 1)[u]]
    elif u == 0:
        ref = q_ref.at[d, 1, b - 1] if b else qr_ref.at[d]
    else:
        ref = q_ref.at[d, u - 1, b]
    if v == 0:
        return jnp.concatenate([ref[0:32, :], ref[96:128, :]], 0)
    return ref[64 * v - 32 : 64 * v + 32, :]


def field_rows(q_ref, qd_ref, qr_ref, a, t, u, v):
    return jnp.concatenate([field_tile(q_ref, qd_ref, qr_ref, a, b, t, u, v) for b in range(8)], 0)


def first_kernel(
    x_ref, xd_ref, xr_ref, xc_ref, sel_ref, k_ref,
    h_ref, q_out, qd_ref, qr_ref, last_ref, side_ref, end_ref,
    x_slabs, q_ref, w_ref, wide, came, went,
):
    def load(d):
        return pltpu.make_async_copy(x_ref.at[:, :, d], x_slabs.at[d], came.at[d])

    def store(d):
        return pltpu.make_async_copy(q_ref.at[d], q_out.at[d], went.at[d])

    for d in range(8):
        load(d).start()
    sel = sel_ref[...]
    qd_ref[0] = spread(sel, xc_ref[...])
    for k in range(16):
        qd_ref[k + 1] = spread(sel, xd_ref[k])
    for k in range(8):
        qr_ref[k] = spread(sel, xr_ref[k])
    w_ref[...] = jnp.zeros_like(w_ref)
    for k in range(27):
        w_ref[k * 128 : k * 128 + 64, 0:128] = k_ref[k]
        w_ref[k * 128 + 64 : k * 128 + 128, 128:256] = k_ref[k]

    @pl.loop(0, 8)
    def slab(d):
        load(d).wait()
        wide[:, 0:16, :] = x_slabs[d].reshape(128, 16, 128).astype(F32)
        for k in range(8):
            both = spread(sel, jnp.concatenate([row(wide, 2 * k), row(wide, 2 * k + 1)], 0))
            for p in range(2):
                q_ref[d, p, k] = both[:, 128 * p : 128 * p + 128]
        store(d).start()

    for a in range(4):
        taps = [field_rows(q_ref, qd_ref, qr_ref, a, t, u, v) for t in range(3) for u in range(3) for v in range(3)]
        pre = dot(jnp.concatenate(taps, 1), w_ref[...])
        out = jnp.where(pre > 0, pre, 0.3 * pre).astype(BF).reshape(8, 64, 256)
        h_ref[a] = out
        side_ref[a] = out[7]
        if a == 3:
            last_ref[...] = out
            end_ref[...] = out[7]
    for d in range(8):
        store(d).wait()


def first(x, xd, xr, xc, sel, kernel):
    anywhere = pl.BlockSpec(memory_space=pl.ANY)
    return pl.pallas_call(
        first_kernel,
        in_specs=[anywhere] + vmem(5),
        out_specs=vmem(1) + [anywhere] + vmem(5),
        out_shape=(
            jax.ShapeDtypeStruct((4, 8, 64, 256), BF),
            jax.ShapeDtypeStruct((8, 2, 8, 160, 128), BF),
            jax.ShapeDtypeStruct((17, 160, 128), BF),
            jax.ShapeDtypeStruct((8, 160, 128), BF),
            jax.ShapeDtypeStruct((8, 64, 256), BF),
            jax.ShapeDtypeStruct((4, 64, 256), BF),
            jax.ShapeDtypeStruct((64, 256), BF),
        ),
        scratch_shapes=[
            pltpu.VMEM((8, 2, 64, 16, 128), BF),
            pltpu.VMEM((8, 2, 8, 160, 128), BF),
            pltpu.VMEM((27 * 128, 256), BF),
            pltpu.VMEM((128, PITCH, 128), F32),
            pltpu.SemaphoreType.DMA((8,)),
            pltpu.SemaphoreType.DMA((8,)),
        ],
        compiler_params=params(54),
        cost_estimate=cost(60, 200),
        name="first_layer",
    )(x, xd, xr, xc, sel, kernel)


def hidden_part(h_ref, hd_ref, hr_ref, hc_ref, a, b):
    if a < 0 and b < 0:
        return hc_ref
    if a < 0:
        return hd_ref.at[b]
    if b < 0:
        return hr_ref.at[a]
    return h_ref.at[a, b]


def shift_rows(value, by):
    wide = pltpu.roll(value.astype(F32), by % 32, 0)
    row = lax.broadcasted_iota(jnp.int32, wide.shape, 0)
    keep = row >= by if by > 0 else row < 32 + by
    return jnp.where(keep, wide, 0.0).astype(BF)


def hidden_shifts(parts, hs_ref):
    for a in range(-1, 4):
        for b in range(-1, 8):
            hs_ref[a + 1, b + 1] = shift_rows(hidden_part(*parts, a, b)[32:64, :], 1)


def hidden_rows(parts, hs_ref, t, u, v):
    pieces = []
    for n in range(2):
        for a in range(2):
            for b in range(4):
                i, j = 2 * a + t - 1, 2 * b + u - 1
                cut = slice(128 * n, 128 * n + 128)
                if v == 0:
                    pieces.append(hs_ref[i + 1, j + 1, :, cut])
                else:
                    pieces.append(hidden_part(*parts, i, j)[32 * (v - 1) : 32 * v, cut])
    return jnp.concatenate(pieces, 0)


WEIGHT = pltpu.VMEM((8, 864, 128), BF)


def whole_weight(core_ref, mine_ref, other_ref, w_ref):
    even = core_ref[0] == 0
    for k in range(27):
        mine, other = (ref[:, 16 * k : 16 * k + 16, :].astype(F32) for ref in (mine_ref, other_ref))
        w_ref[:, 32 * k : 32 * k + 16, :] = jnp.where(even, mine, other).astype(BF)
        w_ref[:, 32 * k + 16 : 32 * k + 32, :] = jnp.where(even, other, mine).astype(BF)


def tap_weight(w_ref, k):
    return w_ref[:, 32 * k : 32 * k + 32, :].reshape(256, 128)


def eye(size):
    rows = lax.broadcasted_iota(jnp.int32, (size, size), 0)
    return (rows == lax.broadcasted_iota(jnp.int32, (size, size), 1)).astype(F32).astype(BF)


def second_kernel(
    core_ref, h_ref, hd_ref, hr_ref, hc_ref, m_ref, o_ref, act_ref, delta_ref, turned_ref, last_ref, side_ref, w_ref, hs_ref
):
    parts = (h_ref, hd_ref, hr_ref, hc_ref)
    hidden_shifts(parts, hs_ref)
    whole_weight(core_ref, m_ref, o_ref, w_ref)
    keys = [(t, u, v) for t in range(3) for u in range(3) for v in range(3)]
    left = jnp.concatenate([hidden_rows(parts, hs_ref, *key) for key in keys], 1)
    right = jnp.concatenate([tap_weight(w_ref, k) for k in range(27)], 1)
    pre = dot(left, right, LANES)
    act = jnp.where(pre > 0, pre, 0.3 * pre).astype(BF)
    slope = jnp.where(pre > 0, 1.0, 0.3).astype(F32)
    small, large = eye(128), eye(256)
    for n in range(2):
        for a in range(2):
            at = 256 * n + 128 * a
            rows = slice(at, at + 128)
            some = slice(64 * a + 32 * n, 32 + 64 * a + 32 * n)
            act_ref[:, some, :] = dot(large, act[rows], LANES).astype(BF).reshape(8, 32, 128)
            some = slice(432 + 64 * a + 32 * n, 464 + 64 * a + 32 * n)
            came = dot(small, m_ref[:, some, :].reshape(256, 128), LANES)
            delta = (came * slope[rows]).astype(BF)
            delta_ref[n, a] = delta.reshape(4, 32, 256)
            side_ref[n, a] = delta[0:32]
            if a == 0:
                last_ref[n] = delta.reshape(4, 32, 256)
            turned_ref[:, rows] = dot(large, delta, LANES).astype(BF)


def second(core, h, hd, hr, hc, mine, other):
    return pl.pallas_call(
        second_kernel,
        in_specs=[SCALAR] + vmem(6),
        out_specs=vmem(5),
        out_shape=(
            jax.ShapeDtypeStruct((8, 128, 128), BF),
            jax.ShapeDtypeStruct((2, 2, 4, 32, 256), BF),
            jax.ShapeDtypeStruct((256, 512), BF),
            jax.ShapeDtypeStruct((2, 4, 32, 256), BF),
            jax.ShapeDtypeStruct((2, 2, 32, 256), BF),
        ),
        scratch_shapes=[WEIGHT, pltpu.VMEM((5, 9, 32, 256), BF)],
        compiler_params=params(16),
        cost_estimate=cost(1, 4),
        name="second_layer",
    )(core, h, hd, hr, hc, mine, other)


def second_grad_kernel(core_ref, h_ref, hd_ref, hr_ref, hc_ref, turned_ref, keep_ref, send_ref, hs_ref):
    parts = (h_ref, hd_ref, hr_ref, hc_ref)
    hidden_shifts(parts, hs_ref)
    turned = turned_ref[...]
    even = core_ref[0] == 0
    keys = [(t, u, v) for t in range(3) for u in range(3) for v in range(3)]
    for k in range(0, 27, 2):
        some = keys[k : k + 2]
        right = jnp.concatenate([hidden_rows(parts, hs_ref, *key) for key in some], 1)
        both = dot(turned, right)
        for p in range(len(some)):
            one = both[:, 128 * p : 128 * p + 128].reshape(8, 2, 16, 128)
            low, high = one[:, 0], one[:, 1]
            spot = ((k + p) // 4, slice(None), slice(16 * ((k + p) % 4), 16 * ((k + p) % 4) + 16))
            keep_ref[spot] = jnp.where(even, low, high).astype(BF)
            send_ref[spot] = jnp.where(even, high, low).astype(BF)
    for ref in (keep_ref, send_ref):
        ref[6, :, 48:64] = jnp.zeros((8, 16, 128), BF)
        ref[7] = jnp.zeros((8, 64, 128), BF)


def second_grad(core, h, hd, hr, hc, turned):
    return pl.pallas_call(
        second_grad_kernel,
        in_specs=[SCALAR] + vmem(5),
        out_specs=vmem(2),
        out_shape=(jax.ShapeDtypeStruct((8, 8, 64, 128), BF),) * 2,
        scratch_shapes=[pltpu.VMEM((5, 9, 32, 256), BF)],
        compiler_params=params(16),
        cost_estimate=cost(1, 4),
        name="second_kernel_grad",
    )(core, h, hd, hr, hc, turned)


def delta_part(d_ref, dd_ref, dr_ref, n, a, b):
    if a > 1:
        return dd_ref.at[n, b]
    if b > 3:
        return dr_ref.at[n, a]
    return d_ref.at[n, a, b]


INNER = [(a, b) for a in range(3) for b in range(7) if (a, b) != (2, 6)]
OUTER = [(3, b) for b in range(8)] + [(0, 7), (1, 7), (2, 7), (2, 6)]


def back_rows(parts, ds_ref, w_ref, h_ref, d_ref, places):
    nothing = jnp.zeros((256, 128), BF)
    choice = (((1, 0),), ((2, 0), (0, 1)))
    for pa in range(2):
        for pb in range(2):
            some = [(a // 2, b // 2) for a, b in places if (a % 2, b % 2) == (pa, pb)]
            left, right = [], []
            for t, i in choice[pa]:
                for u, j in choice[pb]:
                    spots = [(n, a + i, b + j) for n in range(2) for a, b in some]
                    left.append(jnp.concatenate([delta_part(*parts, *spot)[...] for spot in spots], 0))
                    left.append(jnp.concatenate([ds_ref[spot] for spot in spots], 0))
                    k = 9 * t + 3 * u
                    right.append(jnp.concatenate([tap_weight(w_ref, k + 1), tap_weight(w_ref, k + 2)], 1))
                    right.append(jnp.concatenate([nothing, tap_weight(w_ref, k)], 1))
            back = dot(jnp.concatenate(left, 1), jnp.concatenate(right, 0))
            for n in range(2):
                for x, (a, b) in enumerate(some):
                    at = 32 * (n * len(some) + x)
                    place = 2 * a + pa, 2 * b + pb
                    for pc in range(2):
                        rows, cut = slice(32 * pc, 32 * pc + 32), slice(128 * n, 128 * n + 128)
                        slope = jnp.where(h_ref[(*place, rows, cut)].astype(F32) > 0, 1.0, 0.3)
                        value = back[at : at + 32, 128 * pc : 128 * pc + 128]
                        d_ref[places.index(place), rows, cut] = (value * slope).astype(BF)


def grad_rows(d_ref, fields, places):
    turned = dot(eye(256), d_ref[...].reshape(64 * len(places), 256), LANES).astype(BF)
    keys = [(t, u, v) for t in range(3) for u in range(3) for v in range(3)]
    lane = lax.broadcasted_iota(jnp.int32, (128, 128), 1)
    for k in range(0, 27, 2):
        some = keys[k : k + 2]
        right = [jnp.concatenate([field_tile(*fields, *place, *key) for place in places], 0) for key in some]
        both = dot(turned, jnp.concatenate(right, 1))
        one = both[0:128, 0:128] + pltpu.roll(both[128:256, 0:128], 64, 1)
        if len(some) == 2:
            two = both[128:256, 128:256] + pltpu.roll(both[0:128, 128:256], 64, 1)
        else:
            two = jnp.zeros_like(one)
        yield k, jnp.where(lane < 64, one, two).T


def inner_kernel(core_ref, d_ref, m_ref, o_ref, h_ref, q_ref, qd_ref, qr_ref, out_ref, w_ref, ds_ref, one_ref):
    whole_weight(core_ref, m_ref, o_ref, w_ref)
    for n in range(2):
        for a in range(2):
            for b in range(4):
                ds_ref[n, a, b] = shift_rows(d_ref[n, a, b], -1)
    parts = (d_ref, None, None)
    back_rows(parts, ds_ref, w_ref, h_ref, one_ref, INNER)
    for k, rows in grad_rows(one_ref, (q_ref, qd_ref, qr_ref), INNER):
        out_ref[k // 2] = rows


def inner(core, d, mine, other, h, q, qd, qr):
    return pl.pallas_call(
        inner_kernel,
        in_specs=[SCALAR] + vmem(7),
        out_specs=vmem(1)[0],
        out_shape=jax.ShapeDtypeStruct((14, 128, 128), F32),
        scratch_shapes=[WEIGHT, pltpu.VMEM((2, 2, 4, 32, 256), BF), pltpu.VMEM((len(INNER), 64, 256), BF)],
        compiler_params=params(16),
        cost_estimate=cost(4, 9),
        name="first_kernel_grad_inner",
    )(core, d, mine, other, h, q, qd, qr)


def outer_kernel(
    core_ref, d_ref, dd_ref, dr_ref, m_ref, o_ref, h_ref, q_ref, qd_ref, qr_ref, sum_ref,
    keep_ref, send_ref, w_ref, ds_ref, one_ref,
):
    whole_weight(core_ref, m_ref, o_ref, w_ref)
    parts = (d_ref, dd_ref, dr_ref)
    for n in range(2):
        for a in range(3):
            for b in range(5):
                ds_ref[n, a, b] = shift_rows(delta_part(*parts, n, a, b)[...], -1)
    back_rows(parts, ds_ref, w_ref, h_ref, one_ref, OUTER)
    even = core_ref[0] == 0
    for k, rows in grad_rows(one_ref, (q_ref, qd_ref, qr_ref), OUTER):
        rows = rows + sum_ref[k // 2]
        for j in range(4):
            low, high = rows[32 * j : 32 * j + 16], rows[32 * j + 16 : 32 * j + 32]
            spot = (k // 4, 2 * (k % 4) + j)
            keep_ref[spot] = jnp.where(even, low, high).astype(BF)
            send_ref[spot] = jnp.where(even, high, low).astype(BF)
    for ref in (keep_ref, send_ref):
        ref[7] = jnp.zeros((8, 16, 128), BF)


def outer(core, d, dd, dr, mine, other, h, q, qd, qr, partial):
    return pl.pallas_call(
        outer_kernel,
        in_specs=[SCALAR] + vmem(10),
        out_specs=vmem(2),
        out_shape=(jax.ShapeDtypeStruct((8, 8, 16, 128), BF),) * 2,
        scratch_shapes=[WEIGHT, pltpu.VMEM((2, 3, 5, 32, 256), BF), pltpu.VMEM((len(OUTER), 64, 256), BF)],
        compiler_params=params(16),
        cost_estimate=cost(2, 9),
        name="first_kernel_grad",
    )(core, d, dd, dr, mine, other, h, q, qd, qr, partial)


SPACE = ("y_lo", "z", "core")
FILT = ("y_hi", "x")
SLABS = ("y_lo", "z")
CHIPS = ("y_lo", "z", "y_hi", "x")


def exchange(value, axes):
    return lax.all_to_all(value, axes, 0, 0, tiled=True)


def everywhere(value, axes):
    devices = lax.axis_size(axes)
    return exchange(jnp.broadcast_to(value[None], (devices,) + value.shape), axes)


def total(pieces):
    return jnp.sum(pieces.astype(F32), 0).astype(BF)


def paired(keep, send):
    came = lax.ppermute(send, "core", [(0, 1), (1, 0)])
    return (keep.astype(F32) + came.astype(F32)).astype(BF)


def shifted(value, depth, height):
    deep, high = lax.axis_size(SPACE), lax.axis_size(FILT)
    pairs = [
        (i * high + j, (i + depth) * high + j + height)
        for i in range(deep)
        for j in range(high)
        if 0 <= i + depth < deep and 0 <= j + height < high
    ]
    return lax.ppermute(value, SPACE + FILT, pairs)


def body(inputs, kernel_one, kernel_two, cotangent):
    core = lax.axis_index("core").reshape(1)
    sel = jnp.asarray(selection(), BF)
    own = jnp.transpose(kernel_two, (0, 1, 2, 4, 3)).reshape(864, 128)
    parts = jnp.transpose(cotangent.reshape(2, 32, 2, 8, 128), (3, 2, 0, 1, 4)).reshape(8, 128, 128)
    mixed = mix(core, own, parts)

    side, last = rims_of(inputs)
    xr = shifted(side, 0, 1)
    xd = shifted(last, 1, 0)
    xc = shifted(last[7], 1, 1)
    mixed, _ = lax.optimization_barrier((mixed, last))
    mixed = exchange(mixed, FILT)
    h, q, qd, qr, last, side, end = first(inputs, xd, xr, xc, sel, kernel_one.reshape(27, 64, 128))
    mixed, end = lax.optimization_barrier((mixed, end))
    other = lax.ppermute(mixed, "core", [(0, 1), (1, 0)])
    hr = shifted(side, 0, 1)
    hd = shifted(last, 1, 0)
    hc = shifted(end, 1, 1)
    act, delta, turned, last, side = second(core, h, hd, hr, hc, mixed, other)
    dr = shifted(side, 0, -1)
    partial = inner(core, delta, mixed, other, h, q, qd, qr)
    dr, partial = lax.optimization_barrier((dr, partial))
    dd = shifted(jnp.concatenate([last, dr[:, :1]], 1), -1, 0)
    two = second_grad(core, h, hd, hr, hc, turned)
    two, dd = lax.optimization_barrier((two, dd))
    two = paired(*two)
    one = paired(*outer(core, delta, dd, dr, mixed, other, h, q, qd, qr, partial))

    both = jnp.concatenate([two, one], 2).reshape(64, 80, 128)
    both = total(exchange(both, CHIPS))
    one = jnp.broadcast_to(both[None, 64:], (8, 16, 128))
    came = exchange(jnp.concatenate([act, one], 1), FILT)
    mine = everywhere(jnp.concatenate([both[:64], came[:, 128:].reshape(128, 128)], 0), SLABS)
    other = lax.ppermute(mine, "core", [(0, 1), (1, 0)])
    even = lax.axis_index("core") == 0
    full = jnp.stack([jnp.where(even, mine, other), jnp.where(even, other, mine)], 1)
    two = full[:, :, :64].reshape(8, 2, 4, 16, 128)
    two = jnp.transpose(two, (0, 2, 1, 3, 4)).reshape(1024, 128)[:864].reshape(3, 3, 3, 32, 128)
    grad_two = jnp.transpose(two, (0, 1, 2, 4, 3)).astype(F32)
    one = full[:, :, 64:].reshape(8, 2, 8, 16, 128)
    one = jnp.transpose(one, (0, 2, 1, 3, 4)).reshape(2048, 128)[:1728]
    grad_one = one.reshape(3, 3, 3, 64, 128).astype(F32)

    act = came[:, :128].reshape(8, 2, 2, 32, 128)
    activation = jnp.transpose(act, (2, 3, 1, 0, 4)).reshape(cotangent.shape)
    return (activation, grad_one, grad_two)


def solution(mesh):
    fine = jax.sharding.Mesh(mesh.devices.reshape(2, 4, 2, 2, 4), ("y_lo", "z", "core", "y_hi", "x"))
    in_specs = (
        P(None, None, SPACE, FILT, None),
        P(),
        P(None, None, None, None, FILT),
        P(None, FILT, SPACE, None),
    )
    out_specs = (P(None, FILT, SPACE, None), P(), P(None, None, None, None, FILT))
    return jax.shard_map(body, mesh=fine, in_specs=in_specs, out_specs=out_specs, check_vma=False)
```

```python
import jax
import jax.numpy as jnp
import numpy as np
from jax import lax
from jax.experimental import pallas as pl
from jax.experimental.pallas import tpu as pltpu
from jax.sharding import PartitionSpec as P

BF = jnp.bfloat16
F32 = jnp.float32
MIB = 1 << 20
LANES = (((1,), (1,)), ((), ()))
PLAIN = (((1,), (0,)), ((), ()))


def params(mib):
    return pltpu.CompilerParams(vmem_limit_bytes=mib * MIB)


def cost(gigaflops, mib):
    return pl.CostEstimate(flops=gigaflops << 30, bytes_accessed=mib * MIB, transcendentals=0)


def vmem(count):
    return [pl.BlockSpec(memory_space=pltpu.VMEM)] * count


SCALAR = pl.BlockSpec(memory_space=pltpu.SMEM)


def dot(a, b, dims=PLAIN):
    return lax.dot_general(a, b, dims, preferred_element_type=F32)


def selection():
    column = 2 * (np.arange(64) % 32) + np.arange(64) // 32
    wanted = np.concatenate([2 * column[:32] - 1, 2 * column, 2 * column + 1])
    return (wanted[:, None] == np.arange(128)[None, :]).astype(np.float32)


def spread(sel, rows):
    return dot(sel, rows, LANES).astype(BF)


PITCH = 24


def slab_rows(x_ref, d, wide):
    wide[:, 0:16, :] = x_ref[:, :, d].reshape(128, 16, 128).astype(F32)


def row(wide, h):
    return wide.reshape(128 * PITCH, 128)[pl.ds(h, 128, stride=PITCH), :].astype(BF)


def rims_kernel(x_ref, side_ref, last_ref, wide):
    for d in range(8):
        slab_rows(x_ref, d, wide)
        side_ref[d] = row(wide, 15)
    for k in range(8):
        last_ref[k] = row(wide, 2 * k + 1)
        last_ref[8 + k] = row(wide, 2 * k)


def rims_of(inputs):
    return pl.pallas_call(
        rims_kernel,
        in_specs=vmem(1),
        out_specs=vmem(2),
        out_shape=(jax.ShapeDtypeStruct((8, 128, 128), BF), jax.ShapeDtypeStruct((16, 128, 128), BF)),
        scratch_shapes=[pltpu.VMEM((128, PITCH, 128), F32)],
        compiler_params=params(16),
        cost_estimate=cost(0, 6),
        name="input_rims",
    )(inputs)


def mix_kernel(core_ref, own_ref, parts_ref, out_ref):
    even = core_ref[0] == 0
    for k in range(27):
        low, high = own_ref[32 * k : 32 * k + 16], own_ref[32 * k + 16 : 32 * k + 32]
        half = jnp.where(even, low.astype(F32), high.astype(F32)).astype(BF)
        for g in range(8):
            out_ref[g, 16 * k : 16 * k + 16] = half
    for g in range(8):
        out_ref[g, 432:560] = parts_ref[g]


def mix(core, own, parts):
    return pl.pallas_call(
        mix_kernel,
        in_specs=[SCALAR] + vmem(2),
        out_specs=vmem(1)[0],
        out_shape=jax.ShapeDtypeStruct((8, 560, 128), BF),
        compiler_params=params(16),
        cost_estimate=cost(0, 3),
        name="weights_and_cotangent",
    )(core, own, parts)


def field_tile(q_ref, qd_ref, qr_ref, corner_ref, a, b, t, u, v):
    d = 2 * a + t - 1
    if d < 0:
        at = (b, 9 + b, b + 1)[u]
        ref = corner_ref if at == 0 and corner_ref is not None else qd_ref.at[at]
    elif u == 0:
        ref = q_ref.at[d, 1, b - 1] if b else qr_ref.at[d]
    else:
        ref = q_ref.at[d, u - 1, b]
    if v == 0:
        return jnp.concatenate([ref[0:32, :], ref[96:128, :]], 0)
    return ref[64 * v - 32 : 64 * v + 32, :]


def field_rows(q_ref, qd_ref, qr_ref, a, t, u, v):
    return jnp.concatenate([field_tile(q_ref, qd_ref, qr_ref, None, a, b, t, u, v) for b in range(8)], 0)


def first_kernel(
    x_ref, xd_ref, xr_ref, sel_ref, k_ref,
    h_ref, q_out, qd_ref, qr_ref, last_ref, side_ref, end_ref, open_ref,
    x_slabs, q_ref, w_ref, wide, came, went,
):
    def load(d):
        return pltpu.make_async_copy(x_ref.at[:, :, d], x_slabs.at[d], came.at[d])

    def store(d):
        return pltpu.make_async_copy(q_ref.at[d], q_out.at[d], went.at[d])

    for d in range(8):
        load(d).start()
    sel = sel_ref[...]
    qd_ref[0] = jnp.zeros((160, 128), BF)
    last_ref[8] = jnp.concatenate([xr_ref[7, 0:64], xr_ref[7, 64:128]], 1)
    for k in range(16):
        qd_ref[k + 1] = spread(sel, xd_ref[k])
    for k in range(8):
        qr_ref[k] = spread(sel, xr_ref[k])
    w_ref[...] = jnp.zeros_like(w_ref)
    for k in range(27):
        w_ref[k * 128 : k * 128 + 64, 0:128] = k_ref[k]
        w_ref[k * 128 + 64 : k * 128 + 128, 128:256] = k_ref[k]

    @pl.loop(0, 8)
    def slab(d):
        load(d).wait()
        wide[:, 0:16, :] = x_slabs[d].reshape(128, 16, 128).astype(F32)
        for k in range(8):
            both = spread(sel, jnp.concatenate([row(wide, 2 * k), row(wide, 2 * k + 1)], 0))
            for p in range(2):
                q_ref[d, p, k] = both[:, 128 * p : 128 * p + 128]
        store(d).start()

    for a in range(4):
        taps = [field_rows(q_ref, qd_ref, qr_ref, a, t, u, v) for t in range(3) for u in range(3) for v in range(3)]
        pre = dot(jnp.concatenate(taps, 1), w_ref[...])
        out = jnp.where(pre > 0, pre, 0.3 * pre).astype(BF).reshape(8, 64, 256)
        h_ref[a] = out
        side_ref[a] = out[7]
        if a == 3:
            last_ref[0:8] = out
            end_ref[...] = out[7]
        if a == 0:
            open_ref[...] = pre[0:64]
    for d in range(8):
        store(d).wait()


def first(x, xd, xr, sel, kernel):
    anywhere = pl.BlockSpec(memory_space=pl.ANY)
    return pl.pallas_call(
        first_kernel,
        in_specs=[anywhere] + vmem(4),
        out_specs=vmem(1) + [anywhere] + vmem(6),
        out_shape=(
            jax.ShapeDtypeStruct((4, 8, 64, 256), BF),
            jax.ShapeDtypeStruct((8, 2, 8, 160, 128), BF),
            jax.ShapeDtypeStruct((17, 160, 128), BF),
            jax.ShapeDtypeStruct((8, 160, 128), BF),
            jax.ShapeDtypeStruct((9, 64, 256), BF),
            jax.ShapeDtypeStruct((4, 64, 256), BF),
            jax.ShapeDtypeStruct((64, 256), BF),
            jax.ShapeDtypeStruct((64, 256), F32),
        ),
        scratch_shapes=[
            pltpu.VMEM((8, 2, 64, 16, 128), BF),
            pltpu.VMEM((8, 2, 8, 160, 128), BF),
            pltpu.VMEM((27 * 128, 256), BF),
            pltpu.VMEM((128, PITCH, 128), F32),
            pltpu.SemaphoreType.DMA((8,)),
            pltpu.SemaphoreType.DMA((8,)),
        ],
        compiler_params=params(54),
        cost_estimate=cost(60, 200),
        name="first_layer",
    )(x, xd, xr, sel, kernel)


def hidden_part(h_ref, hd_ref, hr_ref, hc_ref, a, b):
    if a < 0 and b < 0:
        return hc_ref
    if a < 0:
        return hd_ref.at[b]
    if b < 0:
        return hr_ref.at[a]
    return h_ref.at[a, b]


def shift_rows(value, by):
    wide = pltpu.roll(value.astype(F32), by % 32, 0)
    row = lax.broadcasted_iota(jnp.int32, wide.shape, 0)
    keep = row >= by if by > 0 else row < 32 + by
    return jnp.where(keep, wide, 0.0).astype(BF)


def hidden_shifts(parts, hs_ref):
    for a in range(-1, 4):
        for b in range(-1, 8):
            hs_ref[a + 1, b + 1] = shift_rows(hidden_part(*parts, a, b)[32:64, :], 1)


def hidden_rows(parts, hs_ref, t, u, v):
    pieces = []
    for n in range(2):
        for a in range(2):
            for b in range(4):
                i, j = 2 * a + t - 1, 2 * b + u - 1
                cut = slice(128 * n, 128 * n + 128)
                if v == 0:
                    pieces.append(hs_ref[i + 1, j + 1, :, cut])
                else:
                    pieces.append(hidden_part(*parts, i, j)[32 * (v - 1) : 32 * v, cut])
    return jnp.concatenate(pieces, 0)


WEIGHT = pltpu.VMEM((8, 864, 128), BF)


def whole_weight(core_ref, mine_ref, other_ref, w_ref):
    even = core_ref[0] == 0
    for k in range(27):
        mine, other = (ref[:, 16 * k : 16 * k + 16, :].astype(F32) for ref in (mine_ref, other_ref))
        w_ref[:, 32 * k : 32 * k + 16, :] = jnp.where(even, mine, other).astype(BF)
        w_ref[:, 32 * k + 16 : 32 * k + 32, :] = jnp.where(even, other, mine).astype(BF)


def tap_weight(w_ref, k):
    return w_ref[:, 32 * k : 32 * k + 32, :].reshape(256, 128)


def eye(size):
    rows = lax.broadcasted_iota(jnp.int32, (size, size), 0)
    return (rows == lax.broadcasted_iota(jnp.int32, (size, size), 1)).astype(F32).astype(BF)


def second_kernel(
    core_ref, h_in, hd_ref, hr_ref, hc_ref, m_ref, o_ref, sel_ref, k_ref, open_ref,
    act_ref, delta_ref, turned_ref, last_ref, side_ref, h_ref, corner_ref, w_ref, hs_ref,
):
    corner = spread(sel_ref[...], jnp.concatenate([hd_ref[8, :, 0:128], hd_ref[8, :, 128:256]], 0))
    corner_ref[...] = corner
    taps = jnp.concatenate([jnp.concatenate([corner[0:32], corner[96:128]], 0), corner[32:96], corner[96:160]], 1)
    nothing = jnp.zeros((64, 128), BF)
    spaced = []
    for k in range(3):
        spaced.append(jnp.concatenate([k_ref[k], nothing], 1))
        spaced.append(jnp.concatenate([nothing, k_ref[k]], 1))
    pre = open_ref[...] + dot(taps, jnp.concatenate(spaced, 0))
    h_ref[...] = h_in[...]
    h_ref[0, 0] = jnp.where(pre > 0, pre, 0.3 * pre).astype(BF)
    parts = (h_ref, hd_ref, hr_ref, hc_ref)
    hidden_shifts(parts, hs_ref)
    whole_weight(core_ref, m_ref, o_ref, w_ref)
    keys = [(t, u, v) for t in range(3) for u in range(3) for v in range(3)]
    left = jnp.concatenate([hidden_rows(parts, hs_ref, *key) for key in keys], 1)
    right = jnp.concatenate([tap_weight(w_ref, k) for k in range(27)], 1)
    pre = dot(left, right, LANES)
    act = jnp.where(pre > 0, pre, 0.3 * pre).astype(BF)
    slope = jnp.where(pre > 0, 1.0, 0.3).astype(F32)
    small, large = eye(128), eye(256)
    for n in range(2):
        for a in range(2):
            at = 256 * n + 128 * a
            rows = slice(at, at + 128)
            some = slice(64 * a + 32 * n, 32 + 64 * a + 32 * n)
            act_ref[:, some, :] = dot(large, act[rows], LANES).astype(BF).reshape(8, 32, 128)
            some = slice(432 + 64 * a + 32 * n, 464 + 64 * a + 32 * n)
            came = dot(small, m_ref[:, some, :].reshape(256, 128), LANES)
            delta = (came * slope[rows]).astype(BF)
            delta_ref[n, a] = delta.reshape(4, 32, 256)
            side_ref[n, a] = delta[0:32]
            if a == 0:
                last_ref[n] = delta.reshape(4, 32, 256)
            turned_ref[:, rows] = dot(large, delta, LANES).astype(BF)


def second(core, h, hd, hr, hc, mine, other, sel, kernel, partial):
    return pl.pallas_call(
        second_kernel,
        in_specs=[SCALAR] + vmem(9),
        out_specs=vmem(7),
        out_shape=(
            jax.ShapeDtypeStruct((8, 128, 128), BF),
            jax.ShapeDtypeStruct((2, 2, 4, 32, 256), BF),
            jax.ShapeDtypeStruct((256, 512), BF),
            jax.ShapeDtypeStruct((2, 4, 32, 256), BF),
            jax.ShapeDtypeStruct((2, 2, 32, 256), BF),
            jax.ShapeDtypeStruct((4, 8, 64, 256), BF),
            jax.ShapeDtypeStruct((160, 128), BF),
        ),
        scratch_shapes=[WEIGHT, pltpu.VMEM((5, 9, 32, 256), BF)],
        compiler_params=params(16),
        cost_estimate=cost(1, 4),
        name="second_layer",
    )(core, h, hd, hr, hc, mine, other, sel, kernel, partial)


def second_grad_kernel(core_ref, h_ref, hd_ref, hr_ref, hc_ref, turned_ref, keep_ref, send_ref, hs_ref):
    parts = (h_ref, hd_ref, hr_ref, hc_ref)
    hidden_shifts(parts, hs_ref)
    turned = turned_ref[...]
    even = core_ref[0] == 0
    keys = [(t, u, v) for t in range(3) for u in range(3) for v in range(3)]
    for k in range(0, 27, 2):
        some = keys[k : k + 2]
        right = jnp.concatenate([hidden_rows(parts, hs_ref, *key) for key in some], 1)
        both = dot(turned, right)
        for p in range(len(some)):
            one = both[:, 128 * p : 128 * p + 128].reshape(8, 2, 16, 128)
            low, high = one[:, 0], one[:, 1]
            spot = ((k + p) // 4, slice(None), slice(16 * ((k + p) % 4), 16 * ((k + p) % 4) + 16))
            keep_ref[spot] = jnp.where(even, low, high).astype(BF)
            send_ref[spot] = jnp.where(even, high, low).astype(BF)
    for ref in (keep_ref, send_ref):
        ref[6, :, 48:64] = jnp.zeros((8, 16, 128), BF)
        ref[7] = jnp.zeros((8, 64, 128), BF)


def second_grad(core, h, hd, hr, hc, turned):
    return pl.pallas_call(
        second_grad_kernel,
        in_specs=[SCALAR] + vmem(5),
        out_specs=vmem(2),
        out_shape=(jax.ShapeDtypeStruct((8, 8, 64, 128), BF),) * 2,
        scratch_shapes=[pltpu.VMEM((5, 9, 32, 256), BF)],
        compiler_params=params(16),
        cost_estimate=cost(1, 4),
        name="second_kernel_grad",
    )(core, h, hd, hr, hc, turned)


def delta_part(d_ref, dd_ref, dr_ref, n, a, b):
    if a > 1:
        return dd_ref.at[n, b]
    if b > 3:
        return dr_ref.at[n, a]
    return d_ref.at[n, a, b]


INNER = [(a, b) for a in range(3) for b in range(7) if (a, b) != (2, 6)]
OUTER = [(3, b) for b in range(8)] + [(0, 7), (1, 7), (2, 7), (2, 6)]


def back_rows(parts, ds_ref, w_ref, h_ref, d_ref, places):
    nothing = jnp.zeros((256, 128), BF)
    choice = (((1, 0),), ((2, 0), (0, 1)))
    for pa in range(2):
        for pb in range(2):
            some = [(a // 2, b // 2) for a, b in places if (a % 2, b % 2) == (pa, pb)]
            left, right = [], []
            for t, i in choice[pa]:
                for u, j in choice[pb]:
                    spots = [(n, a + i, b + j) for n in range(2) for a, b in some]
                    left.append(jnp.concatenate([delta_part(*parts, *spot)[...] for spot in spots], 0))
                    left.append(jnp.concatenate([ds_ref[spot] for spot in spots], 0))
                    k = 9 * t + 3 * u
                    right.append(jnp.concatenate([tap_weight(w_ref, k + 1), tap_weight(w_ref, k + 2)], 1))
                    right.append(jnp.concatenate([nothing, tap_weight(w_ref, k)], 1))
            back = dot(jnp.concatenate(left, 1), jnp.concatenate(right, 0))
            for n in range(2):
                for x, (a, b) in enumerate(some):
                    at = 32 * (n * len(some) + x)
                    place = 2 * a + pa, 2 * b + pb
                    for pc in range(2):
                        rows, cut = slice(32 * pc, 32 * pc + 32), slice(128 * n, 128 * n + 128)
                        slope = jnp.where(h_ref[(*place, rows, cut)].astype(F32) > 0, 1.0, 0.3)
                        value = back[at : at + 32, 128 * pc : 128 * pc + 128]
                        d_ref[places.index(place), rows, cut] = (value * slope).astype(BF)


def grad_rows(d_ref, fields, places):
    turned = dot(eye(256), d_ref[...].reshape(64 * len(places), 256), LANES).astype(BF)
    keys = [(t, u, v) for t in range(3) for u in range(3) for v in range(3)]
    lane = lax.broadcasted_iota(jnp.int32, (128, 128), 1)
    for k in range(0, 27, 2):
        some = keys[k : k + 2]
        right = [jnp.concatenate([field_tile(*fields, *place, *key) for place in places], 0) for key in some]
        both = dot(turned, jnp.concatenate(right, 1))
        one = both[0:128, 0:128] + pltpu.roll(both[128:256, 0:128], 64, 1)
        if len(some) == 2:
            two = both[128:256, 128:256] + pltpu.roll(both[0:128, 128:256], 64, 1)
        else:
            two = jnp.zeros_like(one)
        yield k, jnp.where(lane < 64, one, two).T


def inner_kernel(
    core_ref, d_ref, m_ref, o_ref, h_ref, q_ref, qd_ref, qr_ref, corner_ref, out_ref, w_ref, ds_ref, one_ref
):
    whole_weight(core_ref, m_ref, o_ref, w_ref)
    for n in range(2):
        for a in range(2):
            for b in range(4):
                ds_ref[n, a, b] = shift_rows(d_ref[n, a, b], -1)
    parts = (d_ref, None, None)
    back_rows(parts, ds_ref, w_ref, h_ref, one_ref, INNER)
    for k, rows in grad_rows(one_ref, (q_ref, qd_ref, qr_ref, corner_ref), INNER):
        out_ref[k // 2] = rows


def inner(core, d, mine, other, h, q, qd, qr, corner):
    return pl.pallas_call(
        inner_kernel,
        in_specs=[SCALAR] + vmem(8),
        out_specs=vmem(1)[0],
        out_shape=jax.ShapeDtypeStruct((14, 128, 128), F32),
        scratch_shapes=[WEIGHT, pltpu.VMEM((2, 2, 4, 32, 256), BF), pltpu.VMEM((len(INNER), 64, 256), BF)],
        compiler_params=params(16),
        cost_estimate=cost(4, 9),
        name="first_kernel_grad_inner",
    )(core, d, mine, other, h, q, qd, qr, corner)


def outer_kernel(
    core_ref, d_ref, dd_ref, dr_ref, m_ref, o_ref, h_ref, q_ref, qd_ref, qr_ref, sum_ref,
    keep_ref, send_ref, w_ref, ds_ref, one_ref,
):
    whole_weight(core_ref, m_ref, o_ref, w_ref)
    parts = (d_ref, dd_ref, dr_ref)
    for n in range(2):
        for a in range(3):
            for b in range(5):
                ds_ref[n, a, b] = shift_rows(delta_part(*parts, n, a, b)[...], -1)
    back_rows(parts, ds_ref, w_ref, h_ref, one_ref, OUTER)
    even = core_ref[0] == 0
    for k, rows in grad_rows(one_ref, (q_ref, qd_ref, qr_ref, None), OUTER):
        rows = rows + sum_ref[k // 2]
        for j in range(4):
            low, high = rows[32 * j : 32 * j + 16], rows[32 * j + 16 : 32 * j + 32]
            spot = (k // 4, 2 * (k % 4) + j)
            keep_ref[spot] = jnp.where(even, low, high).astype(BF)
            send_ref[spot] = jnp.where(even, high, low).astype(BF)
    for ref in (keep_ref, send_ref):
        ref[7] = jnp.zeros((8, 16, 128), BF)


def outer(core, d, dd, dr, mine, other, h, q, qd, qr, partial):
    return pl.pallas_call(
        outer_kernel,
        in_specs=[SCALAR] + vmem(10),
        out_specs=vmem(2),
        out_shape=(jax.ShapeDtypeStruct((8, 8, 16, 128), BF),) * 2,
        scratch_shapes=[WEIGHT, pltpu.VMEM((2, 3, 5, 32, 256), BF), pltpu.VMEM((len(OUTER), 64, 256), BF)],
        compiler_params=params(16),
        cost_estimate=cost(2, 9),
        name="first_kernel_grad",
    )(core, d, dd, dr, mine, other, h, q, qd, qr, partial)


SPACE = ("y_lo", "z", "core")
FILT = ("y_hi", "x")
SLABS = ("y_lo", "z")
CHIPS = ("y_lo", "z", "y_hi", "x")


def exchange(value, axes):
    return lax.all_to_all(value, axes, 0, 0, tiled=True)


def everywhere(value, axes):
    devices = lax.axis_size(axes)
    return exchange(jnp.broadcast_to(value[None], (devices,) + value.shape), axes)


def total(pieces):
    return jnp.sum(pieces.astype(F32), 0).astype(BF)


def paired(keep, send):
    came = lax.ppermute(send, "core", [(0, 1), (1, 0)])
    return (keep.astype(F32) + came.astype(F32)).astype(BF)


def shifted(value, depth, height):
    deep, high = lax.axis_size(SPACE), lax.axis_size(FILT)
    pairs = [
        (i * high + j, (i + depth) * high + j + height)
        for i in range(deep)
        for j in range(high)
        if 0 <= i + depth < deep and 0 <= j + height < high
    ]
    return lax.ppermute(value, SPACE + FILT, pairs)


def body(inputs, kernel_one, kernel_two, cotangent):
    core = lax.axis_index("core").reshape(1)
    sel = jnp.asarray(selection(), BF)
    own = jnp.transpose(kernel_two, (0, 1, 2, 4, 3)).reshape(864, 128)
    parts = jnp.transpose(cotangent.reshape(2, 32, 2, 8, 128), (3, 2, 0, 1, 4)).reshape(8, 128, 128)
    mixed = mix(core, own, parts)

    side, last = rims_of(inputs)
    xr = shifted(side, 0, 1)
    xd = shifted(last, 1, 0)
    mixed, _ = lax.optimization_barrier((mixed, last))
    mixed = exchange(mixed, FILT)
    taps = kernel_one.reshape(27, 64, 128)
    h, q, qd, qr, last, side, end, partial = first(inputs, xd, xr, sel, taps)
    mixed, end = lax.optimization_barrier((mixed, end))
    other = lax.ppermute(mixed, "core", [(0, 1), (1, 0)])
    hr = shifted(side, 0, 1)
    hd = shifted(last, 1, 0)
    hc = shifted(end, 1, 1)
    act, delta, turned, last, side, h, corner = second(
        core, h, hd, hr, hc, mixed, other, sel, taps[:3], partial
    )
    dr = shifted(side, 0, -1)
    partial = inner(core, delta, mixed, other, h, q, qd, qr, corner)
    dr, partial = lax.optimization_barrier((dr, partial))
    dd = shifted(jnp.concatenate([last, dr[:, :1]], 1), -1, 0)
    two = second_grad(core, h, hd, hr, hc, turned)
    two, dd = lax.optimization_barrier((two, dd))
    two = paired(*two)
    one = paired(*outer(core, delta, dd, dr, mixed, other, h, q, qd, qr, partial))

    both = jnp.concatenate([two, one], 2).reshape(64, 80, 128)
    both = total(exchange(both, CHIPS))
    one = jnp.broadcast_to(both[None, 64:], (8, 16, 128))
    came = exchange(jnp.concatenate([act, one], 1), FILT)
    mine = everywhere(jnp.concatenate([both[:64], came[:, 128:].reshape(128, 128)], 0), SLABS)
    other = lax.ppermute(mine, "core", [(0, 1), (1, 0)])
    even = lax.axis_index("core") == 0
    full = jnp.stack([jnp.where(even, mine, other), jnp.where(even, other, mine)], 1)
    two = full[:, :, :64].reshape(8, 2, 4, 16, 128)
    two = jnp.transpose(two, (0, 2, 1, 3, 4)).reshape(1024, 128)[:864].reshape(3, 3, 3, 32, 128)
    grad_two = jnp.transpose(two, (0, 1, 2, 4, 3)).astype(F32)
    one = full[:, :, 64:].reshape(8, 2, 8, 16, 128)
    one = jnp.transpose(one, (0, 2, 1, 3, 4)).reshape(2048, 128)[:1728]
    grad_one = one.reshape(3, 3, 3, 64, 128).astype(F32)

    act = came[:, :128].reshape(8, 2, 2, 32, 128)
    activation = jnp.transpose(act, (2, 3, 1, 0, 4)).reshape(cotangent.shape)
    return (activation, grad_one, grad_two)


def solution(mesh):
    fine = jax.sharding.Mesh(mesh.devices.reshape(2, 4, 2, 2, 4), ("y_lo", "z", "core", "y_hi", "x"))
    in_specs = (
        P(None, None, SPACE, FILT, None),
        P(),
        P(None, None, None, None, FILT),
        P(None, FILT, SPACE, None),
    )
    out_specs = (P(None, FILT, SPACE, None), P(), P(None, None, None, None, FILT))
    return jax.shard_map(body, mesh=fine, in_specs=in_specs, out_specs=out_specs, check_vma=False)
```

```python
import jax
import jax.numpy as jnp
import numpy as np
from jax import lax
from jax.experimental import pallas as pl
from jax.experimental.pallas import tpu as pltpu
from jax.sharding import PartitionSpec as P

BF = jnp.bfloat16
F32 = jnp.float32
MIB = 1 << 20
LANES = (((1,), (1,)), ((), ()))
PLAIN = (((1,), (0,)), ((), ()))


def params(mib):
    return pltpu.CompilerParams(vmem_limit_bytes=mib * MIB)


def cost(gigaflops, mib):
    return pl.CostEstimate(flops=gigaflops << 30, bytes_accessed=mib * MIB, transcendentals=0)


def vmem(count):
    return [pl.BlockSpec(memory_space=pltpu.VMEM)] * count


SCALAR = pl.BlockSpec(memory_space=pltpu.SMEM)


def dot(a, b, dims=PLAIN):
    return lax.dot_general(a, b, dims, preferred_element_type=F32)


def selection():
    column = 2 * (np.arange(64) % 32) + np.arange(64) // 32
    wanted = np.concatenate([2 * column[:32] - 1, 2 * column, 2 * column + 1])
    return (wanted[:, None] == np.arange(128)[None, :]).astype(np.float32)


def spread(sel, rows):
    return dot(sel, rows, LANES).astype(BF)


PITCH = 24


def slab_rows(x_ref, d, wide):
    wide[:, 0:16, :] = x_ref[:, :, d].reshape(128, 16, 128).astype(F32)


def row(wide, h):
    return wide.reshape(128 * PITCH, 128)[pl.ds(h, 128, stride=PITCH), :].astype(BF)


def rims_kernel(x_ref, side_ref, last_ref, wide):
    for d in range(8):
        slab_rows(x_ref, d, wide)
        side_ref[d] = row(wide, 15)
    for k in range(8):
        last_ref[k] = row(wide, 2 * k + 1)
        last_ref[8 + k] = row(wide, 2 * k)


def rims_of(inputs):
    return pl.pallas_call(
        rims_kernel,
        in_specs=vmem(1),
        out_specs=vmem(2),
        out_shape=(jax.ShapeDtypeStruct((8, 128, 128), BF), jax.ShapeDtypeStruct((16, 128, 128), BF)),
        scratch_shapes=[pltpu.VMEM((128, PITCH, 128), F32)],
        compiler_params=params(16),
        cost_estimate=cost(0, 6),
        name="input_rims",
    )(inputs)


def mix_kernel(core_ref, own_ref, parts_ref, out_ref):
    even = core_ref[0] == 0
    for k in range(27):
        low, high = own_ref[32 * k : 32 * k + 16], own_ref[32 * k + 16 : 32 * k + 32]
        half = jnp.where(even, low.astype(F32), high.astype(F32)).astype(BF)
        for g in range(8):
            out_ref[g, 16 * k : 16 * k + 16] = half
    for g in range(8):
        out_ref[g, 432:560] = parts_ref[g]


def mix(core, own, parts):
    return pl.pallas_call(
        mix_kernel,
        in_specs=[SCALAR] + vmem(2),
        out_specs=vmem(1)[0],
        out_shape=jax.ShapeDtypeStruct((8, 560, 128), BF),
        compiler_params=params(16),
        cost_estimate=cost(0, 3),
        name="weights_and_cotangent",
    )(core, own, parts)


def field_tile(q_ref, qd_ref, qr_ref, corner_ref, a, b, t, u, v):
    d = 2 * a + t - 1
    if d < 0:
        at = (b, 9 + b, b + 1)[u]
        ref = corner_ref if at == 0 and corner_ref is not None else qd_ref.at[at]
    elif u == 0:
        ref = q_ref.at[d, 1, b - 1] if b else qr_ref.at[d]
    else:
        ref = q_ref.at[d, u - 1, b]
    if v == 0:
        return jnp.concatenate([ref[0:32, :], ref[96:128, :]], 0)
    return ref[64 * v - 32 : 64 * v + 32, :]


def field_rows(q_ref, qd_ref, qr_ref, a, t, u, v):
    return jnp.concatenate([field_tile(q_ref, qd_ref, qr_ref, None, a, b, t, u, v) for b in range(8)], 0)


def first_kernel(
    x_ref, xd_ref, xr_ref, sel_ref, k_ref,
    h_ref, q_out, qd_ref, qr_ref, last_ref, side_ref, end_ref, open_ref,
    x_slabs, q_ref, w_ref, wide, came, went,
):
    def load(d):
        return pltpu.make_async_copy(x_ref.at[:, :, d], x_slabs.at[d], came.at[d])

    def store(d):
        return pltpu.make_async_copy(q_ref.at[d], q_out.at[d], went.at[d])

    for d in range(8):
        load(d).start()
    sel = sel_ref[...]
    qd_ref[0] = jnp.zeros((160, 128), BF)
    last_ref[8] = jnp.concatenate([xr_ref[7, 0:64], xr_ref[7, 64:128]], 1)
    for k in range(16):
        qd_ref[k + 1] = spread(sel, xd_ref[k])
    for k in range(8):
        qr_ref[k] = spread(sel, xr_ref[k])
    w_ref[...] = jnp.zeros_like(w_ref)
    for k in range(27):
        w_ref[k * 128 : k * 128 + 64, 0:128] = k_ref[k]
        w_ref[k * 128 + 64 : k * 128 + 128, 128:256] = k_ref[k]

    @pl.loop(0, 8)
    def slab(d):
        load(d).wait()
        wide[:, 0:16, :] = x_slabs[d].reshape(128, 16, 128).astype(F32)
        for k in range(8):
            both = spread(sel, jnp.concatenate([row(wide, 2 * k), row(wide, 2 * k + 1)], 0))
            for p in range(2):
                q_ref[d, p, k] = both[:, 128 * p : 128 * p + 128]
        store(d).start()

    for a in range(4):
        taps = [field_rows(q_ref, qd_ref, qr_ref, a, t, u, v) for t in range(3) for u in range(3) for v in range(3)]
        pre = dot(jnp.concatenate(taps, 1), w_ref[...])
        out = jnp.where(pre > 0, pre, 0.3 * pre).astype(BF).reshape(8, 64, 256)
        h_ref[a] = out
        side_ref[a] = out[7]
        if a == 3:
            last_ref[0:8] = out
            end_ref[...] = out[7]
        if a == 0:
            open_ref[...] = pre[0:64]
    for d in range(8):
        store(d).wait()


def first(x, xd, xr, sel, kernel):
    anywhere = pl.BlockSpec(memory_space=pl.ANY)
    return pl.pallas_call(
        first_kernel,
        in_specs=[anywhere] + vmem(4),
        out_specs=vmem(1) + [anywhere] + vmem(6),
        out_shape=(
            jax.ShapeDtypeStruct((4, 8, 64, 256), BF),
            jax.ShapeDtypeStruct((8, 2, 8, 160, 128), BF),
            jax.ShapeDtypeStruct((17, 160, 128), BF),
            jax.ShapeDtypeStruct((8, 160, 128), BF),
            jax.ShapeDtypeStruct((9, 64, 256), BF),
            jax.ShapeDtypeStruct((4, 64, 256), BF),
            jax.ShapeDtypeStruct((64, 256), BF),
            jax.ShapeDtypeStruct((64, 256), F32),
        ),
        scratch_shapes=[
            pltpu.VMEM((8, 2, 64, 16, 128), BF),
            pltpu.VMEM((8, 2, 8, 160, 128), BF),
            pltpu.VMEM((27 * 128, 256), BF),
            pltpu.VMEM((128, PITCH, 128), F32),
            pltpu.SemaphoreType.DMA((8,)),
            pltpu.SemaphoreType.DMA((8,)),
        ],
        compiler_params=params(54),
        cost_estimate=cost(60, 200),
        name="first_layer",
    )(x, xd, xr, sel, kernel)


def hidden_part(h_ref, hd_ref, hr_ref, hc_ref, a, b):
    if a < 0 and b < 0:
        return hc_ref
    if a < 0:
        return hd_ref.at[b]
    if b < 0:
        return hr_ref.at[a]
    return h_ref.at[a, b]


def shift_rows(value, by):
    wide = pltpu.roll(value.astype(F32), by % 32, 0)
    row = lax.broadcasted_iota(jnp.int32, wide.shape, 0)
    keep = row >= by if by > 0 else row < 32 + by
    return jnp.where(keep, wide, 0.0).astype(BF)


def hidden_shifts(parts, hs_ref):
    for a in range(-1, 4):
        for b in range(-1, 8):
            hs_ref[a + 1, b + 1] = shift_rows(hidden_part(*parts, a, b)[32:64, :], 1)


def hidden_rows(parts, hs_ref, t, u, v):
    pieces = []
    for n in range(2):
        for a in range(2):
            for b in range(4):
                i, j = 2 * a + t - 1, 2 * b + u - 1
                cut = slice(128 * n, 128 * n + 128)
                if v == 0:
                    pieces.append(hs_ref[i + 1, j + 1, :, cut])
                else:
                    pieces.append(hidden_part(*parts, i, j)[32 * (v - 1) : 32 * v, cut])
    return jnp.concatenate(pieces, 0)


WEIGHT = pltpu.VMEM((8, 864, 128), BF)


def whole_weight(core_ref, mine_ref, other_ref, w_ref):
    even = core_ref[0] == 0
    for k in range(27):
        mine, other = (ref[:, 16 * k : 16 * k + 16, :].astype(F32) for ref in (mine_ref, other_ref))
        w_ref[:, 32 * k : 32 * k + 16, :] = jnp.where(even, mine, other).astype(BF)
        w_ref[:, 32 * k + 16 : 32 * k + 32, :] = jnp.where(even, other, mine).astype(BF)


def tap_weight(w_ref, k):
    return w_ref[:, 32 * k : 32 * k + 32, :].reshape(256, 128)


def eye(size):
    rows = lax.broadcasted_iota(jnp.int32, (size, size), 0)
    return (rows == lax.broadcasted_iota(jnp.int32, (size, size), 1)).astype(F32).astype(BF)


def second_kernel(
    core_ref, h_in, hd_ref, hr_ref, hc_ref, m_ref, o_ref, sel_ref, k_ref, open_ref,
    act_ref, delta_ref, turned_ref, last_ref, side_ref, h_ref, corner_ref, w_ref, hs_ref,
):
    corner = spread(sel_ref[...], jnp.concatenate([hd_ref[8, :, 0:128], hd_ref[8, :, 128:256]], 0))
    corner_ref[...] = corner
    taps = jnp.concatenate([jnp.concatenate([corner[0:32], corner[96:128]], 0), corner[32:96], corner[96:160]], 1)
    nothing = jnp.zeros((64, 128), BF)
    spaced = []
    for k in range(3):
        spaced.append(jnp.concatenate([k_ref[k], nothing], 1))
        spaced.append(jnp.concatenate([nothing, k_ref[k]], 1))
    pre = open_ref[...] + dot(taps, jnp.concatenate(spaced, 0))
    h_ref[...] = h_in[...]
    h_ref[0, 0] = jnp.where(pre > 0, pre, 0.3 * pre).astype(BF)
    parts = (h_ref, hd_ref, hr_ref, hc_ref)
    hidden_shifts(parts, hs_ref)
    whole_weight(core_ref, m_ref, o_ref, w_ref)
    keys = [(t, u, v) for t in range(3) for u in range(3) for v in range(3)]
    left = jnp.concatenate([hidden_rows(parts, hs_ref, *key) for key in keys], 1)
    right = jnp.concatenate([tap_weight(w_ref, k) for k in range(27)], 1)
    pre = dot(left, right, LANES)
    act = jnp.where(pre > 0, pre, 0.3 * pre).astype(BF)
    slope = jnp.where(pre > 0, 1.0, 0.3).astype(F32)
    small, large = eye(128), eye(256)
    for n in range(2):
        for a in range(2):
            at = 256 * n + 128 * a
            rows = slice(at, at + 128)
            some = slice(64 * a + 32 * n, 32 + 64 * a + 32 * n)
            act_ref[:, some, :] = dot(large, act[rows], LANES).astype(BF).reshape(8, 32, 128)
            some = slice(432 + 64 * a + 32 * n, 464 + 64 * a + 32 * n)
            came = dot(small, m_ref[:, some, :].reshape(256, 128), LANES)
            delta = (came * slope[rows]).astype(BF)
            delta_ref[n, a] = delta.reshape(4, 32, 256)
            side_ref[n, a] = delta[0:32]
            if a == 0:
                last_ref[n] = delta.reshape(4, 32, 256)
            turned_ref[:, rows] = dot(large, delta, LANES).astype(BF)


def second(core, h, hd, hr, hc, mine, other, sel, kernel, partial):
    return pl.pallas_call(
        second_kernel,
        in_specs=[SCALAR] + vmem(9),
        out_specs=vmem(7),
        out_shape=(
            jax.ShapeDtypeStruct((8, 128, 128), BF),
            jax.ShapeDtypeStruct((2, 2, 4, 32, 256), BF),
            jax.ShapeDtypeStruct((256, 512), BF),
            jax.ShapeDtypeStruct((2, 4, 32, 256), BF),
            jax.ShapeDtypeStruct((2, 2, 32, 256), BF),
            jax.ShapeDtypeStruct((4, 8, 64, 256), BF),
            jax.ShapeDtypeStruct((160, 128), BF),
        ),
        scratch_shapes=[WEIGHT, pltpu.VMEM((5, 9, 32, 256), BF)],
        compiler_params=params(16),
        cost_estimate=cost(10, 40),
        name="second_layer",
    )(core, h, hd, hr, hc, mine, other, sel, kernel, partial)


def second_grad_kernel(core_ref, h_ref, hd_ref, hr_ref, hc_ref, turned_ref, keep_ref, send_ref, hs_ref):
    parts = (h_ref, hd_ref, hr_ref, hc_ref)
    hidden_shifts(parts, hs_ref)
    turned = turned_ref[...]
    even = core_ref[0] == 0
    keys = [(t, u, v) for t in range(3) for u in range(3) for v in range(3)]
    for k in range(0, 27, 2):
        some = keys[k : k + 2]
        right = jnp.concatenate([hidden_rows(parts, hs_ref, *key) for key in some], 1)
        both = dot(turned, right)
        for p in range(len(some)):
            one = both[:, 128 * p : 128 * p + 128].reshape(8, 2, 16, 128)
            low, high = one[:, 0], one[:, 1]
            spot = ((k + p) // 4, slice(None), slice(16 * ((k + p) % 4), 16 * ((k + p) % 4) + 16))
            keep_ref[spot] = jnp.where(even, low, high).astype(BF)
            send_ref[spot] = jnp.where(even, high, low).astype(BF)
    for ref in (keep_ref, send_ref):
        ref[6, :, 48:64] = jnp.zeros((8, 16, 128), BF)
        ref[7] = jnp.zeros((8, 64, 128), BF)


def second_grad(core, h, hd, hr, hc, turned):
    return pl.pallas_call(
        second_grad_kernel,
        in_specs=[SCALAR] + vmem(5),
        out_specs=vmem(2),
        out_shape=(jax.ShapeDtypeStruct((8, 8, 64, 128), BF),) * 2,
        scratch_shapes=[pltpu.VMEM((5, 9, 32, 256), BF)],
        compiler_params=params(16),
        cost_estimate=cost(1, 4),
        name="second_kernel_grad",
    )(core, h, hd, hr, hc, turned)


def delta_part(d_ref, dd_ref, dr_ref, n, a, b):
    if a > 1:
        return dd_ref.at[n, b]
    if b > 3:
        return dr_ref.at[n, a]
    return d_ref.at[n, a, b]


INNER = [(a, b) for a in range(3) for b in range(7) if (a, b) != (2, 6)]
OUTER = [(3, b) for b in range(8)] + [(0, 7), (1, 7), (2, 7), (2, 6)]


def back_rows(parts, ds_ref, w_ref, h_ref, d_ref, places):
    nothing = jnp.zeros((256, 128), BF)
    choice = (((1, 0),), ((2, 0), (0, 1)))
    for pa in range(2):
        for pb in range(2):
            some = [(a // 2, b // 2) for a, b in places if (a % 2, b % 2) == (pa, pb)]
            left, right = [], []
            for t, i in choice[pa]:
                for u, j in choice[pb]:
                    spots = [(n, a + i, b + j) for n in range(2) for a, b in some]
                    left.append(jnp.concatenate([delta_part(*parts, *spot)[...] for spot in spots], 0))
                    left.append(jnp.concatenate([ds_ref[spot] for spot in spots], 0))
                    k = 9 * t + 3 * u
                    right.append(jnp.concatenate([tap_weight(w_ref, k + 1), tap_weight(w_ref, k + 2)], 1))
                    right.append(jnp.concatenate([nothing, tap_weight(w_ref, k)], 1))
            back = dot(jnp.concatenate(left, 1), jnp.concatenate(right, 0))
            for n in range(2):
                for x, (a, b) in enumerate(some):
                    at = 32 * (n * len(some) + x)
                    place = 2 * a + pa, 2 * b + pb
                    for pc in range(2):
                        rows, cut = slice(32 * pc, 32 * pc + 32), slice(128 * n, 128 * n + 128)
                        slope = jnp.where(h_ref[(*place, rows, cut)].astype(F32) > 0, 1.0, 0.3)
                        value = back[at : at + 32, 128 * pc : 128 * pc + 128]
                        d_ref[places.index(place), rows, cut] = (value * slope).astype(BF)


def grad_rows(d_ref, fields, places):
    turned = dot(eye(256), d_ref[...].reshape(64 * len(places), 256), LANES).astype(BF)
    keys = [(t, u, v) for t in range(3) for u in range(3) for v in range(3)]
    lane = lax.broadcasted_iota(jnp.int32, (128, 128), 1)
    for k in range(0, 27, 2):
        some = keys[k : k + 2]
        right = [jnp.concatenate([field_tile(*fields, *place, *key) for place in places], 0) for key in some]
        both = dot(turned, jnp.concatenate(right, 1))
        one = both[0:128, 0:128] + pltpu.roll(both[128:256, 0:128], 64, 1)
        if len(some) == 2:
            two = both[128:256, 128:256] + pltpu.roll(both[0:128, 128:256], 64, 1)
        else:
            two = jnp.zeros_like(one)
        yield k, jnp.where(lane < 64, one, two).T


def inner_kernel(
    core_ref, d_ref, m_ref, o_ref, h_ref, q_ref, qd_ref, qr_ref, corner_ref, out_ref, w_ref, ds_ref, one_ref
):
    whole_weight(core_ref, m_ref, o_ref, w_ref)
    for n in range(2):
        for a in range(2):
            for b in range(4):
                ds_ref[n, a, b] = shift_rows(d_ref[n, a, b], -1)
    parts = (d_ref, None, None)
    back_rows(parts, ds_ref, w_ref, h_ref, one_ref, INNER)
    for k, rows in grad_rows(one_ref, (q_ref, qd_ref, qr_ref, corner_ref), INNER):
        out_ref[k // 2] = rows


def inner(core, d, mine, other, h, q, qd, qr, corner):
    return pl.pallas_call(
        inner_kernel,
        in_specs=[SCALAR] + vmem(8),
        out_specs=vmem(1)[0],
        out_shape=jax.ShapeDtypeStruct((14, 128, 128), F32),
        scratch_shapes=[WEIGHT, pltpu.VMEM((2, 2, 4, 32, 256), BF), pltpu.VMEM((len(INNER), 64, 256), BF)],
        compiler_params=params(16),
        cost_estimate=cost(4, 9),
        name="first_kernel_grad_inner",
    )(core, d, mine, other, h, q, qd, qr, corner)


def outer_kernel(
    core_ref, d_ref, dd_ref, dr_ref, m_ref, o_ref, h_ref, q_ref, qd_ref, qr_ref, sum_ref,
    keep_ref, send_ref, w_ref, ds_ref, one_ref,
):
    whole_weight(core_ref, m_ref, o_ref, w_ref)
    parts = (d_ref, dd_ref, dr_ref)
    for n in range(2):
        for a in range(3):
            for b in range(5):
                ds_ref[n, a, b] = shift_rows(delta_part(*parts, n, a, b)[...], -1)
    back_rows(parts, ds_ref, w_ref, h_ref, one_ref, OUTER)
    even = core_ref[0] == 0
    for k, rows in grad_rows(one_ref, (q_ref, qd_ref, qr_ref, None), OUTER):
        rows = rows + sum_ref[k // 2]
        for j in range(4):
            low, high = rows[32 * j : 32 * j + 16], rows[32 * j + 16 : 32 * j + 32]
            spot = (k // 4, 2 * (k % 4) + j)
            keep_ref[spot] = jnp.where(even, low, high).astype(BF)
            send_ref[spot] = jnp.where(even, high, low).astype(BF)
    for ref in (keep_ref, send_ref):
        ref[7] = jnp.zeros((8, 16, 128), BF)


def outer(core, d, dd, dr, mine, other, h, q, qd, qr, partial):
    return pl.pallas_call(
        outer_kernel,
        in_specs=[SCALAR] + vmem(10),
        out_specs=vmem(2),
        out_shape=(jax.ShapeDtypeStruct((8, 8, 16, 128), BF),) * 2,
        scratch_shapes=[WEIGHT, pltpu.VMEM((2, 3, 5, 32, 256), BF), pltpu.VMEM((len(OUTER), 64, 256), BF)],
        compiler_params=params(16),
        cost_estimate=cost(2, 9),
        name="first_kernel_grad",
    )(core, d, dd, dr, mine, other, h, q, qd, qr, partial)


SPACE = ("y_lo", "z", "core")
FILT = ("y_hi", "x")
SLABS = ("y_lo", "z")
CHIPS = ("y_lo", "z", "y_hi", "x")


def exchange(value, axes):
    return lax.all_to_all(value, axes, 0, 0, tiled=True)


def everywhere(value, axes):
    devices = lax.axis_size(axes)
    return exchange(jnp.broadcast_to(value[None], (devices,) + value.shape), axes)


def total(pieces):
    return jnp.sum(pieces.astype(F32), 0).astype(BF)


def paired(keep, send):
    came = lax.ppermute(send, "core", [(0, 1), (1, 0)])
    return (keep.astype(F32) + came.astype(F32)).astype(BF)


def shifted(value, depth, height):
    deep, high = lax.axis_size(SPACE), lax.axis_size(FILT)
    pairs = [
        (i * high + j, (i + depth) * high + j + height)
        for i in range(deep)
        for j in range(high)
        if 0 <= i + depth < deep and 0 <= j + height < high
    ]
    return lax.ppermute(value, SPACE + FILT, pairs)


def body(inputs, kernel_one, kernel_two, cotangent):
    core = lax.axis_index("core").reshape(1)
    sel = jnp.asarray(selection(), BF)
    own = jnp.transpose(kernel_two, (0, 1, 2, 4, 3)).reshape(864, 128)
    parts = jnp.transpose(cotangent.reshape(2, 32, 2, 8, 128), (3, 2, 0, 1, 4)).reshape(8, 128, 128)
    mixed = mix(core, own, parts)

    side, last = rims_of(inputs)
    xr = shifted(side, 0, 1)
    xd = shifted(last, 1, 0)
    mixed, _ = lax.optimization_barrier((mixed, last))
    mixed = exchange(mixed, FILT)
    taps = kernel_one.reshape(27, 64, 128)
    h, q, qd, qr, last, side, end, partial = first(inputs, xd, xr, sel, taps)
    mixed, end = lax.optimization_barrier((mixed, end))
    other = lax.ppermute(mixed, "core", [(0, 1), (1, 0)])
    hr = shifted(side, 0, 1)
    hd = shifted(last, 1, 0)
    hc = shifted(end, 1, 1)
    act, delta, turned, last, side, h, corner = second(
        core, h, hd, hr, hc, mixed, other, sel, taps[:3], partial
    )
    dr = shifted(side, 0, -1)
    partial = inner(core, delta, mixed, other, h, q, qd, qr, corner)
    dr, partial = lax.optimization_barrier((dr, partial))
    dd = shifted(jnp.concatenate([last, dr[:, :1]], 1), -1, 0)
    two = second_grad(core, h, hd, hr, hc, turned)
    two, dd = lax.optimization_barrier((two, dd))
    two = paired(*two)
    one = paired(*outer(core, delta, dd, dr, mixed, other, h, q, qd, qr, partial))

    both = jnp.concatenate([two, one], 2).reshape(64, 80, 128)
    both = total(exchange(both, CHIPS))
    one = jnp.broadcast_to(both[None, 64:], (8, 16, 128))
    came = exchange(jnp.concatenate([act, one], 1), FILT)
    mine = everywhere(jnp.concatenate([both[:64], came[:, 128:].reshape(128, 128)], 0), SLABS)
    other = lax.ppermute(mine, "core", [(0, 1), (1, 0)])
    even = lax.axis_index("core") == 0
    full = jnp.stack([jnp.where(even, mine, other), jnp.where(even, other, mine)], 1)
    two = full[:, :, :64].reshape(8, 2, 4, 16, 128)
    two = jnp.transpose(two, (0, 2, 1, 3, 4)).reshape(1024, 128)[:864].reshape(3, 3, 3, 32, 128)
    grad_two = jnp.transpose(two, (0, 1, 2, 4, 3)).astype(F32)
    one = full[:, :, 64:].reshape(8, 2, 8, 16, 128)
    one = jnp.transpose(one, (0, 2, 1, 3, 4)).reshape(2048, 128)[:1728]
    grad_one = one.reshape(3, 3, 3, 64, 128).astype(F32)

    act = came[:, :128].reshape(8, 2, 2, 32, 128)
    activation = jnp.transpose(act, (2, 3, 1, 0, 4)).reshape(cotangent.shape)
    return (activation, grad_one, grad_two)


def solution(mesh):
    fine = jax.sharding.Mesh(mesh.devices.reshape(2, 4, 2, 2, 4), ("y_lo", "z", "core", "y_hi", "x"))
    in_specs = (
        P(None, None, SPACE, FILT, None),
        P(),
        P(None, None, None, None, FILT),
        P(None, FILT, SPACE, None),
    )
    out_specs = (P(None, FILT, SPACE, None), P(), P(None, None, None, None, FILT))
    return jax.shard_map(body, mesh=fine, in_specs=in_specs, out_specs=out_specs, check_vma=False)
```
